256 devices in a mesh: cells: 16 (over y_hi, z), modes: 16 (over y_lo, x, core).
Axes of the slice: x: 4, y: 4 (y_hi: 2, y_lo: 2; y = y_hi * 2 + y_lo), z: 8, core: 2. Of those that a mesh axis runs over, the one named last changes fastest.
Arguments:
- theta: float32 [8192, 32], P('modes'), may hold values from -6 to 6
- basis: bfloat16 [32768, 8192], P('cells', 'modes'), may hold values from -0.0625 to 0.0625
- mean_logk: float32 [32768], P('cells'), may hold values from -3 to 3
- face_mult: float32 [3, 32768], P(None, 'cells'), may hold values from 0.3 to 3
- storage: float32 [32768], P('cells'), may hold values from 0.05 to 0.5
- sources: float32 [32768], P('cells'), may hold values from -6 to 6
- obs_data: float32 [32768], P('cells'), may hold values from -6 to 6
- obs_weight: float32 [32768], P('cells'), may hold values from 0.1 to 1
- fault_pairs: int32 [4096, 2], P('cells'), may hold values from 0 to 2047, as said below
- fault_mult: float32 [4096], P('cells'), may hold values from 0.1 to 1
- noise: float32 [8192, 32], P('modes'), may hold values from -6 to 6
Outputs:
- theta_next: float32 [8192, 32], P('modes')
- grad: float32 [8192, 32], P('modes')
- pressure: float32 [32, 32768], P('modes', 'cells')
The draws below stay inside these ranges and needn't reach their ends.
Inputs may be any that keep to these rules, and one draw needn't show every extreme that they name: `fault_pairs`: each block of 256 slots lists its live connections first; each joins a cell (x, y, z) of the block with (x, y+1, z+s), 1 <= s <= 3; the remaining slots pair a cell with itself. Some block is full in every draw.
All inputs are finite; a program needn't handle non-finite values.
Results may differ from the reference program's by a relative error of at most 0.0047.
Values may be sent and summed in bfloat16 or wider, within the bound.
No kernel may reach another device: no remote copies, remote signals or barrier semaphores. Data moves between devices by JAX's collectives and lax.ppermute only.
A program may use at most 64 MiB of HBM per device.

```python
import math
import jax
import jax.numpy as jnp
from jax import lax

SX = 1
NY = 32
NZ = 64
MODES = 8192
CHAINS = 32
SWEEPS = 6
THROW = 3
NNC_DEV = 256
C_DEV = 2048
NX = 16
CELLS = 32768
NNC_TOT = 4096
N_CELLS = 16


def draw_fault_pairs(key, part):
    keys = jax.random.split(key, 6)
    total = NNC_DEV * N_CELLS
    layer_x = jax.random.randint(keys[0], (total,), 0, SX)
    layer_y = jax.random.randint(keys[1], (total,), 0, NY - 1)
    layer_z = jax.random.randint(keys[2], (total,), 0, NZ - THROW)
    throw_z = jax.random.randint(keys[3], (total,), 1, THROW + 1)
    slot = jnp.arange(total) % NNC_DEV
    block = jnp.arange(total) // NNC_DEV
    layer_x = jnp.where(slot == 0, 0, jnp.where(slot == 1, SX - 1, layer_x))
    layer_y = jnp.where(slot == 0, 0, jnp.where(slot == 1, NY - 2, layer_y))
    layer_z = jnp.where(slot == 0, 0, jnp.where(slot == 1, NZ - 1 - THROW, layer_z))
    throw_z = jnp.where(slot < 2, THROW, throw_z)
    near_cell = (layer_x * NY + layer_y) * NZ + layer_z
    far_cell = (layer_x * NY + layer_y + 1) * NZ + layer_z + throw_z
    live_count = jax.random.randint(keys[4], (N_CELLS,), NNC_DEV // 4, NNC_DEV + 1)
    full_block = jax.random.randint(keys[5], (), 0, N_CELLS)
    live_count = jnp.where(jnp.arange(N_CELLS) == full_block, NNC_DEV, live_count)
    keep = slot < live_count[block]
    far_cell = jnp.where(keep, far_cell, near_cell)
    return jnp.stack([near_cell, far_cell], 1).astype(jnp.int32)


def block_levels(stream_key, shape, shards, low, high):
    level, own = 1.0, jax.random.fold_in(stream_key, 6)
    for dim, parts in shards:
        steps = jnp.exp(jax.random.uniform(jax.random.fold_in(own, dim), (parts,), jnp.float32, low / len(shards), high / len(shards)))
        level = level * jnp.repeat(steps, shape[dim] // parts).reshape([-1 if axis == dim else 1 for axis in range(len(shape))])
    return level


def centred(rng, extent, spread, limit, cuts=(), held_as=jnp.bfloat16):
    factor_of = block_levels(rng, extent, cuts, -0.22, 0.18) if cuts else 1.0
    values = jax.random.normal(rng, extent, jnp.float32) * spread * factor_of
    return jnp.minimum(jnp.maximum(values, -limit), limit).astype(held_as)


def setup_inputs(seed: int = 0) -> dict:
    streams_of = jax.random.split(jax.random.key(seed), 12)
    theta = centred(streams_of[0], (MODES, CHAINS), 1.0, 6.0, ((0, 16),), jnp.float32)
    basis = centred(streams_of[1], (CELLS, MODES), MODES ** -0.5, 0.0625, ((0, 16), (1, 16)))
    mean_logk = centred(streams_of[2], (CELLS,), 0.5, 3.0, ((0, 16),), jnp.float32)
    face_mult = jnp.clip(jnp.exp(math.log(3.0) - 2.3025851 * jax.random.uniform(streams_of[3], (3, CELLS), jnp.float32) ** block_levels(streams_of[3], (3, CELLS), ((1, 16),), -0.2, 0.2)), 0.3, 3.0)
    storage = jnp.clip(jnp.exp(math.log(0.5) - 2.3025851 * jax.random.uniform(streams_of[4], (CELLS,), jnp.float32) ** block_levels(streams_of[4], (CELLS,), ((0, 16),), -0.2, 0.2)), 0.05, 0.5)
    sources = centred(streams_of[5], (CELLS,), 1.0, 6.0, ((0, 16),), jnp.float32)
    obs_data = centred(streams_of[6], (CELLS,), 1.0, 6.0, ((0, 16),), jnp.float32)
    obs_weight = jnp.clip(jnp.exp(math.log(1.0) - 2.3025851 * jax.random.uniform(streams_of[7], (CELLS,), jnp.float32) ** block_levels(streams_of[7], (CELLS,), ((0, 16),), -0.2, 0.2)), 0.1, 1.0)
    fault_pairs = draw_fault_pairs(jax.random.fold_in(streams_of[11], 71), 0)
    fault_mult = jnp.clip(jnp.exp(math.log(1.0) - 2.3025851 * jax.random.uniform(streams_of[9], (NNC_TOT,), jnp.float32) ** block_levels(streams_of[9], (NNC_TOT,), ((0, 16),), -0.2, 0.2)), 0.1, 1.0)
    noise = centred(streams_of[10], (MODES, CHAINS), 1.0, 6.0, ((0, 16),), jnp.float32)
    return dict(theta=theta, basis=basis, mean_logk=mean_logk, face_mult=face_mult, storage=storage, sources=sources, obs_data=obs_data, obs_weight=obs_weight, fault_pairs=fault_pairs, fault_mult=fault_mult, noise=noise)


LOW_EIG = 0.1
HIGH_EIG = 1.9
STEP_SIZE = 0.01

def harmonic(left, right):
    return 2.0 * left * right / (left + right)

def pad_axis(array, axis, before, after):
    widths = [(0, 0)] * array.ndim
    widths[axis] = (before, after)
    return jnp.pad(array, widths)

def transmit(perm_ext, mult_ext, mult_y, mult_z, near_cell, far_cell, fault_mult, depth_y, depth_z):
    chains_n = perm_ext.shape[0]
    layers = perm_ext.shape[1] - 2
    trans_x = harmonic(perm_ext[:, :-1], perm_ext[:, 1:]) * mult_ext[:, :-1]
    perm = perm_ext[:, 1:-1].reshape(chains_n, layers, depth_y, depth_z)
    trans_y = harmonic(perm[:, :, :-1], perm[:, :, 1:]) * mult_y.reshape(1, layers, depth_y, depth_z)[:, :, :-1]
    trans_z = harmonic(perm[..., :-1], perm[..., 1:]) * mult_z.reshape(1, layers, depth_y, depth_z)[..., :-1]
    flat = perm.reshape(chains_n, -1)
    live = fault_mult * (near_cell != far_cell).astype(fault_mult.dtype)
    trans_n = harmonic(flat[:, near_cell], flat[:, far_cell]) * live[None]
    return (trans_x, trans_y, trans_z, trans_n)

def diagonal_of(trans, storage, near_cell, far_cell, depth_y, depth_z):
    trans_x, trans_y, trans_z, trans_n = trans
    chains_n = trans_x.shape[0]
    layers = trans_x.shape[1] - 1
    total = (trans_x[:, 1:] + trans_x[:, :-1]).reshape(chains_n, layers, depth_y, depth_z)
    total = total + pad_axis(trans_y, 2, 0, 1) + pad_axis(trans_y, 2, 1, 0)
    total = total + pad_axis(trans_z, 3, 0, 1) + pad_axis(trans_z, 3, 1, 0)
    total = total.reshape(chains_n, -1)
    total = total.at[:, near_cell].add(trans_n).at[:, far_cell].add(trans_n)
    return total + storage[None]

def operate(field_ext, trans, storage, near_cell, far_cell, depth_y, depth_z):
    trans_x, trans_y, trans_z, trans_n = trans
    chains_n = field_ext.shape[0]
    layers = field_ext.shape[1] - 2
    flux_x = trans_x * (field_ext[:, :-1] - field_ext[:, 1:])
    result = (flux_x[:, 1:] - flux_x[:, :-1]).reshape(chains_n, layers, depth_y, depth_z)
    field = field_ext[:, 1:-1].reshape(chains_n, layers, depth_y, depth_z)
    flux_y = trans_y * (field[:, :, :-1] - field[:, :, 1:])
    result = result + pad_axis(flux_y, 2, 0, 1) - pad_axis(flux_y, 2, 1, 0)
    flux_z = trans_z * (field[..., :-1] - field[..., 1:])
    result = result + pad_axis(flux_z, 3, 0, 1) - pad_axis(flux_z, 3, 1, 0)
    result = result.reshape(chains_n, -1)
    flat = field.reshape(chains_n, -1)
    flux_n = trans_n * (flat[:, near_cell] - flat[:, far_cell])
    result = result.at[:, near_cell].add(flux_n).at[:, far_cell].add(-flux_n)
    return result + storage[None] * flat

def solve(rhs, apply_fn, diag):
    center = 0.5 * (HIGH_EIG + LOW_EIG)
    half = 0.5 * (HIGH_EIG - LOW_EIG)
    sigma = center / half
    resid = rhs / diag
    direction = resid / center
    iterate = jnp.zeros_like(rhs)
    rho = jnp.asarray(1.0 / sigma, dtype=rhs.dtype)

    def sweep_step(sweep, carry):
        iterate, resid, direction, rho = carry
        iterate = iterate + direction
        resid = resid - apply_fn(direction) / diag
        rho_next = 1.0 / (2.0 * sigma - rho)
        direction = rho_next * rho * direction + 2.0 * rho_next / half * resid
        return (iterate, resid, direction, rho_next)
    iterate, resid, direction, rho = lax.fori_loop(0, SWEEPS, sweep_step, (iterate, resid, direction, rho))
    return iterate + direction

def gradient_of(pres_ext, adj_ext, perm_ext, trans, near_cell, far_cell, depth_y, depth_z):
    trans_x, trans_y, trans_z, trans_n = trans
    chains_n = perm_ext.shape[0]
    layers = perm_ext.shape[1] - 2
    coef_x = -(adj_ext[:, :-1] - adj_ext[:, 1:]) * (pres_ext[:, :-1] - pres_ext[:, 1:]) * trans_x / (perm_ext[:, :-1] + perm_ext[:, 1:])
    result = coef_x[:, 1:] * perm_ext[:, 2:] + coef_x[:, :-1] * perm_ext[:, :-2]
    result = result.reshape(chains_n, layers, depth_y, depth_z)
    shape4 = (chains_n, layers, depth_y, depth_z)
    perm = perm_ext[:, 1:-1].reshape(shape4)
    pres = pres_ext[:, 1:-1].reshape(shape4)
    adj = adj_ext[:, 1:-1].reshape(shape4)
    coef_y = -(adj[:, :, :-1] - adj[:, :, 1:]) * (pres[:, :, :-1] - pres[:, :, 1:]) * trans_y / (perm[:, :, :-1] + perm[:, :, 1:])
    result = result + pad_axis(coef_y * perm[:, :, 1:], 2, 0, 1) + pad_axis(coef_y * perm[:, :, :-1], 2, 1, 0)
    coef_z = -(adj[..., :-1] - adj[..., 1:]) * (pres[..., :-1] - pres[..., 1:]) * trans_z / (perm[..., :-1] + perm[..., 1:])
    result = result + pad_axis(coef_z * perm[..., 1:], 3, 0, 1) + pad_axis(coef_z * perm[..., :-1], 3, 1, 0)
    result = result.reshape(chains_n, -1)
    perm_f = perm.reshape(chains_n, -1)
    pres_f = pres.reshape(chains_n, -1)
    adj_f = adj.reshape(chains_n, -1)
    perm_a = perm_f[:, near_cell]
    perm_b = perm_f[:, far_cell]
    coef_n = -(adj_f[:, near_cell] - adj_f[:, far_cell]) * (pres_f[:, near_cell] - pres_f[:, far_cell]) * trans_n / (perm_a + perm_b)
    return result.at[:, near_cell].add(coef_n * perm_b).at[:, far_cell].add(coef_n * perm_a)

def extend_zero(array):
    return jnp.pad(array, ((0, 0), (1, 1), (0, 0)))

def reference(theta, basis, mean_logk, face_mult, storage, sources, obs_data, obs_weight, fault_pairs, fault_mult, noise):
    theta_b = theta.astype(jnp.bfloat16)
    theta_w = theta_b.astype(jnp.float32)
    blocks = basis.reshape(N_CELLS, C_DEV, MODES)

    def field_block(block):
        return jnp.dot(block.astype(jnp.float32), theta_w, precision=lax.Precision.HIGHEST)
    partial_field = lax.map(field_block, blocks).reshape(CELLS, -1)
    logk = mean_logk[None] + partial_field.T
    chains_n = logk.shape[0]
    faces = NY * NZ
    offset = (jnp.arange(NNC_TOT) // NNC_DEV * C_DEV).astype(jnp.int32)
    near_cell = fault_pairs[:, 0].astype(jnp.int32) + offset
    far_cell = fault_pairs[:, 1].astype(jnp.int32) + offset
    perm = jnp.exp(logk).reshape(chains_n, NX, faces)
    perm_ext = extend_zero(perm)
    mult_ext = extend_zero(face_mult[0].reshape(1, NX, faces))
    trans = transmit(perm_ext, mult_ext, face_mult[1], face_mult[2], near_cell, far_cell, fault_mult, NY, NZ)
    diag = diagonal_of(trans, storage, near_cell, far_cell, NY, NZ)

    def apply_fn(field):
        return operate(extend_zero(field.reshape(chains_n, NX, faces)), trans, storage, near_cell, far_cell, NY, NZ)
    rhs = jnp.broadcast_to(sources[None], logk.shape)
    pressure = solve(rhs, apply_fn, diag)
    misfit = obs_weight[None] * (pressure - obs_data[None])
    adjoint = solve(misfit, apply_fn, diag)
    pres_ext = extend_zero(pressure.reshape(chains_n, NX, faces))
    adj_ext = extend_zero(adjoint.reshape(chains_n, NX, faces))
    glogk = gradient_of(pres_ext, adj_ext, perm_ext, trans, near_cell, far_cell, NY, NZ)
    glogk_b = glogk.astype(jnp.bfloat16)
    grad_blocks = jnp.transpose(glogk_b.reshape(chains_n, N_CELLS, C_DEV), (1, 0, 2))

    def grad_step(total, pair):
        gpiece, bpiece = pair
        return (total + jnp.dot(gpiece.astype(jnp.float32), bpiece.astype(jnp.float32), precision=lax.Precision.HIGHEST), None)
    grad_rows, unused = lax.scan(grad_step, jnp.zeros((chains_n, MODES), jnp.float32), (grad_blocks, blocks))
    grad = grad_rows.T
    theta_next = theta - STEP_SIZE * (grad + theta) + math.sqrt(2.0 * STEP_SIZE) * noise
    return (theta_next, grad, pressure)
```

```python
import math

import jax
import jax.numpy as jnp
from jax import lax
from jax.experimental import pallas as pl
from jax.experimental.pallas import tpu as pltpu
from jax.sharding import PartitionSpec as P

NY = 32
NZ = 64
SWEEPS = 6
LAYERS = 16
LANES = 128
ROWS = NY * NZ // LANES
SLOT_ROWS = 2
PIECE = 48
THROWS = 3

LOW_EIG = 0.1
HIGH_EIG = 1.9
STEP_SIZE = 0.01
AXES = ("cells", "modes")
VMEM = pl.BlockSpec(memory_space=pltpu.VMEM)
SMEM = pl.BlockSpec(memory_space=pltpu.SMEM)


def cost(flops, bytes_accessed):
    return pl.CostEstimate(flops=flops, bytes_accessed=bytes_accessed, transcendentals=0)


def chebyshev():
    center = 0.5 * (HIGH_EIG + LOW_EIG)
    half = 0.5 * (HIGH_EIG - LOW_EIG)
    sigma = center / half
    rho = 1.0 / sigma
    factors = []
    for _ in range(SWEEPS):
        rho_next = 1.0 / (2.0 * sigma - rho)
        factors.append((rho_next * rho, 2.0 * rho_next / half))
        rho = rho_next
    return center, factors


CENTER, FACTORS = chebyshev()


def field_kernel(theta_ref, basis_ref, out_ref):
    theta_b = theta_ref[...].astype(jnp.bfloat16)
    part = lax.dot_general(
        theta_b, basis_ref[...], (((1,), (1,)), ((), ())), preferred_element_type=jnp.float32
    )
    for row in range(out_ref.shape[1]):
        out_ref[:, row, :] = part[:, row * LANES : (row + 1) * LANES]


def field_of(theta, basis):
    chains, modes = theta.shape
    steps = 2
    return pl.pallas_call(
        field_kernel,
        grid=(steps,),
        in_specs=[
            pl.BlockSpec((chains, modes), lambda i: (0, 0)),
            pl.BlockSpec((ROWS * LANES // steps, modes), lambda i: (i, 0)),
        ],
        out_specs=pl.BlockSpec((chains, ROWS // steps, LANES), lambda i: (0, i, 0)),
        out_shape=jax.ShapeDtypeStruct((chains, ROWS, LANES), jnp.float32),
        cost_estimate=cost(2 * chains * modes * ROWS * LANES, 2 * modes * ROWS * LANES),
        name="field",
    )(theta, basis)


def left_half():
    return lax.broadcasted_iota(jnp.int32, (ROWS, LANES), 1) < NZ


def swap(a):
    return pltpu.roll(a, NZ, 1)


def span(low, high):
    return low, (high - low) / 65535.0


MULT_SPAN, STORE_SPAN, WELL_SPAN, UNIT_SPAN = (
    span(0.3, 3.0),
    span(0.05, 0.5),
    span(-6.0, 6.0),
    span(0.1, 1.0),
)


def code16(a, within):
    low, step = within
    return ((a - low) * (1.0 / step) + 0.5).astype(jnp.int32) - 32768


def value16(code, within):
    low, step = within
    return (code + 32768).astype(jnp.float32) * step + low


def pack(high, low):
    return (high << 16) | (low & 0xFFFF)


def high16(word):
    return word >> 16


def low16(word):
    return (word << 16) >> 16


def combine_kernel(
    place_ref,
    parts_ref,
    mean_ref,
    face_ref,
    storage_ref,
    sources_ref,
    data_ref,
    weight_ref,
    pairs_ref,
    fault_ref,
    out_ref,
):
    total = jnp.sum(parts_ref[...], axis=0)
    mean = mean_ref[...]
    first, second = total[0] + mean, total[1] + mean
    left = left_half()
    even = jnp.where(left, first, swap(second))
    odd = jnp.where(left, swap(first), second)
    top = jnp.max(jnp.maximum(jnp.abs(even), jnp.abs(odd)), axis=(0, 1), keepdims=True)
    bound = (top * 256.0).astype(jnp.int32) + 1
    factor = (32767.0 * 256.0) / bound.astype(jnp.float32)

    def scaled(a):
        return jnp.floor(a * factor + 0.5).astype(jnp.int32)

    def rows_of(a):
        return jnp.concatenate(
            [a[:, row * LANES : (row + 1) * LANES] for row in range(a.shape[1] // LANES)], 0
        )

    face = face_ref[...]
    mult = [code16(rows_of(face[k : k + 1]), MULT_SPAN) for k in range(3)]
    store = code16(storage_ref[...], STORE_SPAN)
    source = code16(sources_ref[...], WELL_SPAN)
    data = code16(data_ref[...], WELL_SPAN)
    weight = code16(weight_ref[...], UNIT_SPAN)
    near, far = rows_of(pairs_ref[0:1]), rows_of(pairs_ref[1:2])
    code = near * 4 + jnp.where(near == far, 0, far - near - NZ)
    fault = code16(rows_of(fault_ref[...]), UNIT_SPAN)
    bounds = jnp.broadcast_to(bound, (2, LANES))
    zeros = jnp.zeros((2, LANES), jnp.int32)
    forms = (
        [
            pack(mult[0], mult[1]),
            pack(mult[2][0:8], mult[2][8:16]),
            pack(store[0:4], store[4:8]),
            zeros,
            bounds,
        ],
        [
            pack(source, data),
            pack(weight[0:8], weight[8:16]),
            pack(store[8:12], store[12:16]),
            pack(code, fault),
            bounds,
        ],
    )
    forms = [jnp.concatenate(form, 0) for form in forms]
    fixed = jnp.where(place_ref[1] == 0, forms[0], forms[1])
    field = pack(scaled(even), scaled(odd))
    for k in range(out_ref.shape[0]):
        out_ref[k, 0:ROWS] = field
        out_ref[k, ROWS:PIECE] = fixed


def combine(place, parts, *fixed):
    return pl.pallas_call(
        combine_kernel,
        in_specs=[SMEM] + [VMEM] * (1 + len(fixed)),
        out_specs=VMEM,
        out_shape=jax.ShapeDtypeStruct((LAYERS, PIECE, LANES), jnp.int32),
        cost_estimate=cost(2**17, 2**20),
        name="combine",
    )(place, parts, *fixed)


def harmonic(left, right):
    return 2.0 * left * right / (left + right)


def ahead(a, s):
    return pltpu.roll(a, LANES - s, 1)


def behind(a, s):
    return pltpu.roll(a, s, 1)


def up(a):
    return pltpu.roll(a, ROWS - 1, 0)


def down(a):
    return pltpu.roll(a, 1, 0)


def spread(a):
    left, other = left_half(), swap(a)
    return jnp.where(left, a, other), jnp.where(left, other, a)


def neighbours(even, odd, above, below):
    to_even = [above[0], below[0], ahead(even, 1), behind(even, 1), odd, down(odd)]
    to_odd = [above[1], below[1], ahead(odd, 1), behind(odd, 1), up(even), even]
    for s in range(1, THROWS + 1):
        to_even.append(ahead(odd, s))
        to_odd.append(up(ahead(even, s)))
    for s in range(1, THROWS + 1):
        to_even.append(down(behind(odd, s)))
        to_odd.append(behind(even, s))
    return to_even, to_odd


def physics_kernel(
    place_ref,
    own_ref,
    other_ref,
    pressure_ref,
    glogk_ref,
    perm,
    coef,
    inverse,
    local,
    weight,
    data,
    resid,
    field,
    adjoint,
    dir_a,
    dir_b,
):
    here, core = place_ref[0], place_ref[1]
    zeros = jnp.zeros((ROWS, LANES), jnp.float32)
    for pad in (0, LAYERS + 1):
        for k in range(2):
            perm[pad, k] = zeros + 1.0
            field[pad, k] = zeros
            adjoint[pad, k] = zeros
            dir_a[pad, k] = zeros
            dir_b[pad, k] = zeros
    for x in range(LAYERS):
        word = own_ref[x, 0:ROWS]
        factor = own_ref[x, PIECE - 1 : PIECE].astype(jnp.float32) * (1.0 / (32767.0 * 256.0))
        perm[x + 1, 0] = jnp.exp(high16(word).astype(jnp.float32) * factor)
        perm[x + 1, 1] = jnp.exp(low16(word).astype(jnp.float32) * factor)

    lane = lax.broadcasted_iota(jnp.int32, (ROWS, LANES), 1)
    row = lax.broadcasted_iota(jnp.int32, (ROWS, LANES), 0)
    z_inside = (lane & (NZ - 1)) < NZ - 1
    y_inside = row < ROWS - 1
    keys = lax.broadcasted_iota(jnp.int32, (THROWS * ROWS, LANES), 0)
    lanes_of = lax.broadcasted_iota(jnp.int32, (LANES, LANES), 0)

    def prepare(x, carry):
        own, other = own_ref[x, ROWS:PIECE], other_ref[x, ROWS:PIECE]
        first = jnp.where(core == 0, own, other)
        second = jnp.where(core == 0, other, own)
        mult_x = spread(value16(high16(first[0:16]), MULT_SPAN))
        mult_y = spread(value16(low16(first[0:16]), MULT_SPAN))
        halves = (high16(first[16:24]), low16(first[16:24]))
        mult_z = spread(value16(jnp.concatenate(halves, 0), MULT_SPAN))
        store = [op(w[24:28]) for w in (first, second) for op in (high16, low16)]
        storage = spread(value16(jnp.concatenate(store, 0), STORE_SPAN))
        source = spread(value16(high16(second[0:16]), WELL_SPAN))
        obs_data = spread(value16(low16(second[0:16]), WELL_SPAN))
        halves = (high16(second[16:24]), low16(second[16:24]))
        obs_weight = spread(value16(jnp.concatenate(halves, 0), UNIT_SPAN))
        slots = second[28:30]
        faults = jnp.zeros((THROWS * ROWS, LANES), jnp.float32)
        for h in range(SLOT_ROWS):
            code = high16(slots[h : h + 1])
            throw, cell = code & 3, code >> 2
            key = jnp.where(throw > 0, (throw - 1) * ROWS + (cell >> 7), -1)
            amount = value16(low16(slots[h : h + 1]), UNIT_SPAN)
            rows_hot = jnp.where(keys == key, amount, 0.0)
            lanes_hot = jnp.where(lanes_of == (cell & (LANES - 1)), 1.0, 0.0).astype(jnp.bfloat16)
            for _ in range(3):
                piece = rows_hot.astype(jnp.bfloat16)
                faults = faults + lax.dot_general(
                    piece, lanes_hot, (((1,), (1,)), ((), ())), preferred_element_type=jnp.float32
                )
                rows_hot = rows_hot - piece.astype(jnp.float32)
        even, odd = perm[x + 1, 0], perm[x + 1, 1]
        inside = jnp.where(x < LAYERS - 1, 1.0, 0.0)
        xp_even = harmonic(even, perm[x + 2, 0]) * mult_x[0] * inside
        xp_odd = harmonic(odd, perm[x + 2, 1]) * mult_x[1] * inside
        xm_even, xm_odd = carry
        zp_even = jnp.where(z_inside, harmonic(even, ahead(even, 1)) * mult_z[0], 0.0)
        zp_odd = jnp.where(z_inside, harmonic(odd, ahead(odd, 1)) * mult_z[1], 0.0)
        y_even = harmonic(even, odd) * mult_y[0]
        y_odd = jnp.where(y_inside, harmonic(odd, up(even)) * mult_y[1], 0.0)
        to_even = [xp_even, xm_even, zp_even, behind(zp_even, 1), y_even, down(y_odd)]
        to_odd = [xp_odd, xm_odd, zp_odd, behind(zp_odd, 1), y_odd, y_even]
        back_even, back_odd = [], []
        for s in range(1, THROWS + 1):
            fault = spread(faults[(s - 1) * ROWS : s * ROWS])
            fault_even = harmonic(even, ahead(odd, s)) * fault[0]
            fault_odd = harmonic(odd, up(ahead(even, s))) * fault[1]
            to_even.append(fault_even)
            to_odd.append(fault_odd)
            back_even.append(down(behind(fault_odd, s)))
            back_odd.append(behind(fault_even, s))
        to_even += back_even
        to_odd += back_odd

        @pl.when(x == here)
        def _():
            for k in range(12):
                local[k, 0] = to_even[k]
                local[k, 1] = to_odd[k]

        for side, trans in ((0, to_even), (1, to_odd)):
            diag = storage[side]
            for t in trans:
                diag = diag + t
            inv = 1.0 / diag
            inverse[x, side] = inv
            for k in range(12):
                value = trans[k] * inv
                if side == 0 and k in (5, 9, 10, 11):
                    value = up(value)
                if side == 1 and k in (4, 6, 7, 8):
                    value = down(value)
                coef[x, k, side] = value
            weight[x, side] = obs_weight[side]
            data[x, side] = obs_data[side]
            start = source[side] * inv
            resid[x, side] = start
            dir_a[x + 1, side] = start * (1.0 / CENTER)
            field[x + 1, side] = zeros
        return xp_even, xp_odd

    lax.fori_loop(0, LAYERS, prepare, (zeros, zeros))

    def sweep(total, source_dir, target_dir, keep, gain):
        for x in range(LAYERS):
            even, odd = source_dir[x + 1, 0], source_dir[x + 1, 1]
            c = lambda k, side: coef[x, k, side]
            acc_even = c(0, 0) * source_dir[x + 2, 0] + c(1, 0) * source_dir[x, 0]
            acc_odd = c(0, 1) * source_dir[x + 2, 1] + c(1, 1) * source_dir[x, 1]
            acc_even += c(4, 0) * odd
            acc_odd += c(5, 1) * even
            low = c(5, 0) * odd
            high = c(4, 1) * even
            for s in range(1, THROWS + 1):
                even_ahead, odd_ahead = ahead(even, s), ahead(odd, s)
                even_behind, odd_behind = behind(even, s), behind(odd, s)
                if s == 1:
                    acc_even += c(2, 0) * even_ahead + c(3, 0) * even_behind
                    acc_odd += c(2, 1) * odd_ahead + c(3, 1) * odd_behind
                acc_even += c(5 + s, 0) * odd_ahead
                acc_odd += c(8 + s, 1) * even_behind
                low += c(8 + s, 0) * odd_behind
                high += c(5 + s, 1) * even_ahead
            acc_even += down(low)
            acc_odd += up(high)
            for side, own, acc in ((0, even, acc_even), (1, odd, acc_odd)):
                left = resid[x, side] - (own - acc)
                resid[x, side] = left
                total[x + 1, side] = total[x + 1, side] + own
                target_dir[x + 1, side] = keep * own + gain * left

    def solve(total):
        def pair(i, carry):
            def pick(k, j):
                return jnp.where(
                    i == 0,
                    FACTORS[k][j],
                    jnp.where(i == 1, FACTORS[k + 2][j], FACTORS[k + 4][j]),
                ).astype(jnp.float32)

            sweep(total, dir_a, dir_b, pick(0, 0), pick(0, 1))
            sweep(total, dir_b, dir_a, pick(1, 0), pick(1, 1))
            return carry

        lax.fori_loop(0, SWEEPS // 2, pair, 0)

    solve(field)
    for x in range(LAYERS):
        for side in range(2):
            value = field[x + 1, side] + dir_a[x + 1, side]
            field[x + 1, side] = value
            start = weight[x, side] * (value - data[x, side]) * inverse[x, side]
            resid[x, side] = start
            dir_a[x + 1, side] = start * (1.0 / CENTER)
            adjoint[x + 1, side] = zeros
    solve(adjoint)

    def around(ref, extra=None):
        def read(layer):
            pair = [ref[here + layer, 0], ref[here + layer, 1]]
            if extra is not None:
                pair = [pair[k] + extra[here + layer, k] for k in range(2)]
            return pair

        below, mine, above = read(0), read(1), read(2)
        return mine, neighbours(mine[0], mine[1], above, below)

    perm_mine, perm_next = around(perm)
    pres_mine, pres_next = around(field)
    adj_mine, adj_next = around(adjoint, dir_a)
    glogk = []
    for side in range(2):
        total = zeros
        for k in range(12):
            other = perm_next[side][k]
            rate = (
                -(adj_mine[side] - adj_next[side][k])
                * (pres_mine[side] - pres_next[side][k])
                * local[k, side]
                / (perm_mine[side] + other)
            )
            total = total + rate * other
        glogk.append(total)

    def apart(even, odd):
        left = left_half()
        return jnp.where(left, even, swap(odd)), jnp.where(left, swap(even), odd)

    first, second = apart(*pres_mine)
    pressure_ref[0] = first
    pressure_ref[1] = second
    first, second = apart(*glogk)
    first, second = first.astype(jnp.bfloat16), second.astype(jnp.bfloat16)
    for m in range(glogk_ref.shape[0]):
        glogk_ref[m, 0] = first
        glogk_ref[m, 1] = second


def physics(place, own, other, copies):
    f32 = jnp.float32

    def buffer(*lead):
        return pltpu.VMEM((*lead, ROWS, LANES), f32)

    padded = LAYERS + 2
    return pl.pallas_call(
        physics_kernel,
        in_specs=[SMEM] + [VMEM] * 2,
        out_specs=[VMEM, VMEM],
        out_shape=[
            jax.ShapeDtypeStruct((2, ROWS, LANES), f32),
            jax.ShapeDtypeStruct((copies, 2, ROWS, LANES), jnp.bfloat16),
        ],
        scratch_shapes=[
            buffer(padded, 2),
            buffer(LAYERS, 12, 2),
            buffer(LAYERS, 2),
            buffer(12, 2),
            buffer(LAYERS, 2),
            buffer(LAYERS, 2),
            buffer(LAYERS, 2),
            buffer(padded, 2),
            buffer(padded, 2),
            buffer(padded, 2),
            buffer(padded, 2),
        ],
        compiler_params=pltpu.CompilerParams(vmem_limit_bytes=24 * 2**20),
        cost_estimate=cost(2**32, 2**24),
        name="physics",
    )(place, own, other)


def gradient_kernel(glogk_ref, basis_ref, out_ref, rows):
    chains = out_ref.shape[0]
    values = glogk_ref[...].astype(jnp.float32).reshape(chains, ROWS, LANES)
    rows[...] = values
    for row in range(ROWS):
        left = rows[:, row, :].astype(jnp.bfloat16)
        part = jnp.dot(
            left,
            basis_ref[row * LANES : (row + 1) * LANES, :],
            preferred_element_type=jnp.float32,
        )
        if row == 0:
            out_ref[...] = part
        else:
            out_ref[...] += part


def gradient_of(glogk, basis):
    chains = glogk.shape[0] * glogk.shape[1]
    return pl.pallas_call(
        gradient_kernel,
        in_specs=[VMEM, VMEM],
        out_specs=VMEM,
        out_shape=jax.ShapeDtypeStruct((chains, basis.shape[1]), jnp.float32),
        scratch_shapes=[pltpu.VMEM((chains, ROWS, LANES), jnp.float32)],
        compiler_params=pltpu.CompilerParams(vmem_limit_bytes=16 * 2**20),
        cost_estimate=cost(2 * chains * basis.size, 2 * basis.size),
        name="gradient",
    )(glogk, basis)


def copies_kernel(one_ref, two_ref, out_ref):
    total = (one_ref[...] + two_ref[...]).astype(jnp.bfloat16)
    for k in range(out_ref.shape[0]):
        out_ref[k] = total


def copies_of(one, two, count):
    return pl.pallas_call(
        copies_kernel,
        in_specs=[VMEM, VMEM],
        out_specs=VMEM,
        out_shape=jax.ShapeDtypeStruct((count, *one.shape), jnp.bfloat16),
        cost_estimate=cost(2**16, 2**19),
        name="copies",
    )(one, two)


def exchange(value, mask, size):
    return lax.ppermute(value, AXES, [(i, i ^ mask) for i in range(size)])


def body(
    theta,
    basis,
    mean_logk,
    face_mult,
    storage,
    sources,
    obs_data,
    obs_weight,
    fault_pairs,
    fault_mult,
    noise,
):
    modes_n, cells_n = lax.axis_size("modes"), lax.axis_size("cells")
    size = cells_n * modes_n
    here = lax.axis_index("cells")
    core = lax.axis_index("modes") & 1
    place = jnp.stack([here, core]).astype(jnp.int32)

    partial_field = field_of(theta.T, basis).reshape(modes_n, 2, ROWS, LANES)
    parts = lax.all_to_all(partial_field, "modes", 0, 0)
    pieces = combine(
        place,
        parts,
        mean_logk.reshape(ROWS, LANES),
        face_mult,
        storage.reshape(ROWS, LANES),
        sources.reshape(ROWS, LANES),
        obs_data.reshape(ROWS, LANES),
        obs_weight.reshape(ROWS, LANES),
        fault_pairs.T,
        fault_mult.reshape(1, SLOT_ROWS * LANES),
    )
    pieces = lax.all_to_all(pieces, "cells", 0, 0)
    others = exchange(pieces, 1, size)
    pressure, glogk = physics(place, pieces, others, modes_n)
    glogk = lax.all_to_all(glogk, "modes", 0, 0)
    grad_rows = gradient_of(glogk, basis)
    half = cells_n // 2
    grad_rows = copies_of(grad_rows, exchange(grad_rows, half * modes_n, size), half)
    groups = [list(range(half)), list(range(half, cells_n))]
    grad_rows = lax.all_to_all(grad_rows, "cells", 0, 0, axis_index_groups=groups)
    grad = jnp.sum(grad_rows.astype(jnp.float32), 0).T
    theta_next = theta - STEP_SIZE * (grad + theta) + math.sqrt(2.0 * STEP_SIZE) * noise
    return (theta_next, grad, pressure.reshape(2, NY * NZ))


def solution(mesh):
    return jax.shard_map(
        body,
        mesh=mesh,
        in_specs=(
            P("modes", None),
            P("cells", "modes"),
            P("cells"),
            P(None, "cells"),
            P("cells"),
            P("cells"),
            P("cells"),
            P("cells"),
            P("cells", None),
            P("cells"),
            P("modes", None),
        ),
        out_specs=(P("modes", None), P("modes", None), P("modes", "cells")),
        check_vma=False,
    )
```

```python
import math

import jax
import jax.numpy as jnp
from jax import lax
from jax.experimental import pallas as pl
from jax.experimental.pallas import tpu as pltpu
from jax.sharding import PartitionSpec as P

NY = 32
NZ = 64
SWEEPS = 6
LAYERS = 16
LANES = 128
ROWS = NY * NZ // LANES
SLOT_ROWS = 2
PIECE = 48
THROWS = 3

LOW_EIG = 0.1
HIGH_EIG = 1.9
STEP_SIZE = 0.01
AXES = ("cells", "modes")
VMEM = pl.BlockSpec(memory_space=pltpu.VMEM)


def place():
    return lax.axis_index("cells"), lax.axis_index("modes") & 1


def cost(flops, bytes_accessed):
    return pl.CostEstimate(flops=flops, bytes_accessed=bytes_accessed, transcendentals=0)


def chebyshev():
    center = 0.5 * (HIGH_EIG + LOW_EIG)
    half = 0.5 * (HIGH_EIG - LOW_EIG)
    sigma = center / half
    rho = 1.0 / sigma
    factors = []
    for _ in range(SWEEPS):
        rho_next = 1.0 / (2.0 * sigma - rho)
        factors.append((rho_next * rho, 2.0 * rho_next / half))
        rho = rho_next
    return center, factors


CENTER, FACTORS = chebyshev()


def field_kernel(theta_hbm, basis_hbm, out_ref, theta, basis, sems):
    steps = sems.shape[0] - 1
    count = basis.shape[0] // steps
    copies = [pltpu.make_async_copy(theta_hbm, theta, sems.at[steps])]
    for step in range(steps):
        rows = pl.ds(step * count, count)
        copies.append(pltpu.make_async_copy(basis_hbm.at[rows], basis.at[rows], sems.at[step]))
    for copy in copies:
        copy.start()
    copies[0].wait()
    theta_b = theta[...].astype(jnp.bfloat16)
    for step in range(steps):
        copies[step + 1].wait()
        part = lax.dot_general(
            theta_b,
            basis[step * count : (step + 1) * count, :],
            (((1,), (1,)), ((), ())),
            preferred_element_type=jnp.float32,
        )
        for row in range(count // LANES):
            out_ref[:, step * (count // LANES) + row, :] = part[:, row * LANES : (row + 1) * LANES]


def field_of(theta, basis):
    chains, modes = theta.shape
    steps = 4
    return pl.pallas_call(
        field_kernel,
        in_specs=[pl.BlockSpec(memory_space=pltpu.HBM)] * 2,
        out_specs=VMEM,
        out_shape=jax.ShapeDtypeStruct((chains, ROWS, LANES), jnp.float32),
        scratch_shapes=[
            pltpu.VMEM(theta.shape, theta.dtype),
            pltpu.VMEM(basis.shape, basis.dtype),
            pltpu.SemaphoreType.DMA((steps + 1,)),
        ],
        cost_estimate=cost(2 * chains * modes * ROWS * LANES, 2 * modes * ROWS * LANES),
        compiler_params=pltpu.CompilerParams(vmem_limit_bytes=8 * 2**20),
        name="field",
    )(
        pltpu.with_memory_space_constraint(theta, pltpu.HBM),
        pltpu.with_memory_space_constraint(basis, pltpu.HBM),
    )


def left_half():
    return lax.broadcasted_iota(jnp.int32, (ROWS, LANES), 1) < NZ


def swap(a):
    return pltpu.roll(a, NZ, 1)


def span(low, high):
    return low, (high - low) / 65535.0


MULT_SPAN, STORE_SPAN, WELL_SPAN, UNIT_SPAN = (
    span(0.3, 3.0),
    span(0.05, 0.5),
    span(-6.0, 6.0),
    span(0.1, 1.0),
)


def code16(a, within):
    low, step = within
    return ((a - low) * (1.0 / step) + 0.5).astype(jnp.int32) - 32768


def value16(code, within):
    low, step = within
    return (code + 32768).astype(jnp.float32) * step + low


def pack(high, low):
    return (high << 16) | (low & 0xFFFF)


def high16(word):
    return word >> 16


def low16(word):
    return (word << 16) >> 16


def combine_kernel(
    parts_ref,
    mean_ref,
    face_ref,
    storage_ref,
    sources_ref,
    data_ref,
    weight_ref,
    pairs_ref,
    fault_ref,
    out_ref,
):
    total = jnp.sum(parts_ref[...], axis=0)
    mean = mean_ref[...]
    first, second = total[0] + mean, total[1] + mean
    left = left_half()
    even = jnp.where(left, first, swap(second))
    odd = jnp.where(left, swap(first), second)
    top = jnp.max(jnp.maximum(jnp.abs(even), jnp.abs(odd)), axis=(0, 1), keepdims=True)
    bound = (top * 256.0).astype(jnp.int32) + 1
    factor = (32767.0 * 256.0) / bound.astype(jnp.float32)

    def scaled(a):
        return jnp.floor(a * factor + 0.5).astype(jnp.int32)

    def rows_of(a):
        return jnp.concatenate(
            [a[:, row * LANES : (row + 1) * LANES] for row in range(a.shape[1] // LANES)], 0
        )

    face = face_ref[...]
    mult = [code16(rows_of(face[k : k + 1]), MULT_SPAN) for k in range(3)]
    store = code16(storage_ref[...], STORE_SPAN)
    source = code16(sources_ref[...], WELL_SPAN)
    data = code16(data_ref[...], WELL_SPAN)
    weight = code16(weight_ref[...], UNIT_SPAN)
    near, far = rows_of(pairs_ref[0:1]), rows_of(pairs_ref[1:2])
    code = near * 4 + jnp.where(near == far, 0, far - near - NZ)
    fault = (rows_of(fault_ref[...]) * 65535.0 + 0.5).astype(jnp.int32) - 32768
    bounds = jnp.broadcast_to(bound, (2, LANES))
    zeros = jnp.zeros((2, LANES), jnp.int32)
    forms = (
        [
            pack(mult[0], mult[1]),
            pack(mult[2][0:8], mult[2][8:16]),
            pack(store[0:4], store[4:8]),
            zeros,
            bounds,
        ],
        [
            pack(source, data),
            pack(weight[0:8], weight[8:16]),
            pack(store[8:12], store[12:16]),
            pack(code, fault),
            bounds,
        ],
    )
    forms = [jnp.concatenate(form, 0) for form in forms]
    fixed = jnp.where(place()[1] == 0, forms[0], forms[1])
    field = pack(scaled(even), scaled(odd))
    for k in range(out_ref.shape[0]):
        out_ref[k, 0:ROWS] = field
        out_ref[k, ROWS:PIECE] = fixed


def combine(parts, *fixed):
    return pl.pallas_call(
        combine_kernel,
        in_specs=[VMEM] * (1 + len(fixed)),
        out_specs=VMEM,
        out_shape=jax.ShapeDtypeStruct((LAYERS, PIECE, LANES), jnp.int32),
        cost_estimate=cost(2**17, 2**20),
        compiler_params=pltpu.CompilerParams(vmem_limit_bytes=4 * 2**20),
        name="combine",
    )(parts, *fixed)


def harmonic(left, right):
    return 2.0 * left * right / (left + right)


def ahead(a, s):
    return pltpu.roll(a, LANES - s, 1)


def behind(a, s):
    return pltpu.roll(a, s, 1)


def up(a):
    return pltpu.roll(a, ROWS - 1, 0)


def down(a):
    return pltpu.roll(a, 1, 0)


def spread(a):
    left, other = left_half(), swap(a)
    return jnp.where(left, a, other), jnp.where(left, other, a)


def neighbours(even, odd, above, below):
    to_even = [above[0], below[0], ahead(even, 1), behind(even, 1), odd, down(odd)]
    to_odd = [above[1], below[1], ahead(odd, 1), behind(odd, 1), up(even), even]
    for s in range(1, THROWS + 1):
        to_even.append(ahead(odd, s))
        to_odd.append(up(ahead(even, s)))
    for s in range(1, THROWS + 1):
        to_even.append(down(behind(odd, s)))
        to_odd.append(behind(even, s))
    return to_even, to_odd


def physics_kernel(
    own_ref,
    other_ref,
    pressure_ref,
    glogk_ref,
    perm,
    coef,
    inverse,
    local,
    fault,
    weight,
    data,
    resid,
    field,
    adjoint,
    dir_a,
    dir_b,
):
    here, core = place()
    zeros = jnp.zeros((ROWS, LANES), jnp.float32)
    for pad in (0, LAYERS + 1):
        for k in range(2):
            perm[pad, k] = zeros + 1.0
            field[pad, k] = zeros
            adjoint[pad, k] = zeros
            dir_a[pad, k] = zeros
            dir_b[pad, k] = zeros
    for x in range(LAYERS):
        word = own_ref[x, 0:ROWS]
        factor = own_ref[x, PIECE - 1 : PIECE].astype(jnp.float32) * (1.0 / (32767.0 * 256.0))
        perm[x + 1, 0] = jnp.exp(high16(word).astype(jnp.float32) * factor)
        perm[x + 1, 1] = jnp.exp(low16(word).astype(jnp.float32) * factor)

    lane = lax.broadcasted_iota(jnp.int32, (ROWS, LANES), 1)
    row = lax.broadcasted_iota(jnp.int32, (ROWS, LANES), 0)
    z_inside = (lane & (NZ - 1)) < NZ - 1
    y_inside = row < ROWS - 1
    keys = lax.broadcasted_iota(jnp.int32, (THROWS * ROWS, SLOT_ROWS * LANES), 0)
    lanes_of = lax.broadcasted_iota(jnp.int32, (LANES, SLOT_ROWS * LANES), 0)

    def join(x):
        own, other = own_ref[x, PIECE - 4 : PIECE - 2], other_ref[x, PIECE - 4 : PIECE - 2]
        slots = jnp.where(core == 0, other, own)
        slots = jnp.concatenate([slots[h : h + 1] for h in range(SLOT_ROWS)], 1)
        code, amount = high16(slots), low16(slots) + 32768
        throw, cell = code & 3, code >> 2
        key = jnp.where(throw > 0, (throw - 1) * ROWS + (cell >> 7), -1)
        hit = keys == key
        parts = [
            jnp.where(hit, part.astype(jnp.float32), 0.0) for part in (amount >> 8, amount & 255)
        ]
        rows_hot = jnp.concatenate(parts, 0).astype(jnp.bfloat16)
        lanes_hot = jnp.where(lanes_of == (cell & (LANES - 1)), 1.0, 0.0).astype(jnp.bfloat16)
        sums = lax.dot_general(
            rows_hot, lanes_hot, (((1,), (1,)), ((), ())), preferred_element_type=jnp.float32
        )
        count = THROWS * ROWS
        total = (sums[:count] * 256.0 + sums[count:]) * (1.0 / 65535.0)
        for s in range(THROWS):
            even, odd = spread(total[s * ROWS : (s + 1) * ROWS])
            fault[x, s, 0] = even
            fault[x, s, 1] = odd

    for x in range(LAYERS):
        join(x)

    def prepare(x, carry):
        own, other = own_ref[x, ROWS:PIECE], other_ref[x, ROWS:PIECE]
        first = jnp.where(core == 0, own, other)
        second = jnp.where(core == 0, other, own)
        mult_x = spread(value16(high16(first[0:16]), MULT_SPAN))
        mult_y = spread(value16(low16(first[0:16]), MULT_SPAN))
        halves = (high16(first[16:24]), low16(first[16:24]))
        mult_z = spread(value16(jnp.concatenate(halves, 0), MULT_SPAN))
        store = [op(w[24:28]) for w in (first, second) for op in (high16, low16)]
        storage = spread(value16(jnp.concatenate(store, 0), STORE_SPAN))
        source = spread(value16(high16(second[0:16]), WELL_SPAN))
        obs_data = spread(value16(low16(second[0:16]), WELL_SPAN))
        halves = (high16(second[16:24]), low16(second[16:24]))
        obs_weight = spread(value16(jnp.concatenate(halves, 0), UNIT_SPAN))
        even, odd = perm[x + 1, 0], perm[x + 1, 1]
        inside = jnp.where(x < LAYERS - 1, 1.0, 0.0)
        xp_even = harmonic(even, perm[x + 2, 0]) * mult_x[0] * inside
        xp_odd = harmonic(odd, perm[x + 2, 1]) * mult_x[1] * inside
        xm_even, xm_odd = carry
        zp_even = jnp.where(z_inside, harmonic(even, ahead(even, 1)) * mult_z[0], 0.0)
        zp_odd = jnp.where(z_inside, harmonic(odd, ahead(odd, 1)) * mult_z[1], 0.0)
        y_even = harmonic(even, odd) * mult_y[0]
        y_odd = jnp.where(y_inside, harmonic(odd, up(even)) * mult_y[1], 0.0)
        to_even = [xp_even, xm_even, zp_even, behind(zp_even, 1), y_even, down(y_odd)]
        to_odd = [xp_odd, xm_odd, zp_odd, behind(zp_odd, 1), y_odd, y_even]
        back_even, back_odd = [], []
        for s in range(1, THROWS + 1):
            fault_even = harmonic(even, ahead(odd, s)) * fault[x, s - 1, 0]
            fault_odd = harmonic(odd, up(ahead(even, s))) * fault[x, s - 1, 1]
            to_even.append(fault_even)
            to_odd.append(fault_odd)
            back_even.append(down(behind(fault_odd, s)))
            back_odd.append(behind(fault_even, s))
        to_even += back_even
        to_odd += back_odd

        @pl.when(x == here)
        def _():
            for k in range(12):
                local[k, 0] = to_even[k]
                local[k, 1] = to_odd[k]

        for side, trans in ((0, to_even), (1, to_odd)):
            diag = storage[side]
            for t in trans:
                diag = diag + t
            inv = 1.0 / diag
            inverse[x, side] = inv
            for k in range(12):
                value = trans[k] * inv
                if side == 0 and k in (5, 9, 10, 11):
                    value = up(value)
                if side == 1 and k in (4, 6, 7, 8):
                    value = down(value)
                coef[x, k, side] = value
            weight[x, side] = obs_weight[side]
            data[x, side] = obs_data[side]
            start = source[side] * inv
            resid[x, side] = start
            dir_a[x + 1, side] = start * (1.0 / CENTER)
            field[x + 1, side] = zeros
        return xp_even, xp_odd

    lax.fori_loop(0, LAYERS, prepare, (zeros, zeros), unroll=4)

    def sweep(total, source_dir, target_dir, keep, gain):
        for x in range(LAYERS):
            even, odd = source_dir[x + 1, 0], source_dir[x + 1, 1]
            c = lambda k, side: coef[x, k, side]
            acc_even = c(0, 0) * source_dir[x + 2, 0] + c(1, 0) * source_dir[x, 0]
            acc_odd = c(0, 1) * source_dir[x + 2, 1] + c(1, 1) * source_dir[x, 1]
            acc_even += c(4, 0) * odd
            acc_odd += c(5, 1) * even
            low = c(5, 0) * odd
            high = c(4, 1) * even
            for s in range(1, THROWS + 1):
                even_ahead, odd_ahead = ahead(even, s), ahead(odd, s)
                even_behind, odd_behind = behind(even, s), behind(odd, s)
                if s == 1:
                    acc_even += c(2, 0) * even_ahead + c(3, 0) * even_behind
                    acc_odd += c(2, 1) * odd_ahead + c(3, 1) * odd_behind
                acc_even += c(5 + s, 0) * odd_ahead
                acc_odd += c(8 + s, 1) * even_behind
                low += c(8 + s, 0) * odd_behind
                high += c(5 + s, 1) * even_ahead
            acc_even += down(low)
            acc_odd += up(high)
            for side, own, acc in ((0, even, acc_even), (1, odd, acc_odd)):
                left = resid[x, side] - (own - acc)
                resid[x, side] = left
                total[x + 1, side] = total[x + 1, side] + own
                target_dir[x + 1, side] = keep * own + gain * left

    def solve(total):
        def pair(i, carry):
            def pick(k, j):
                return jnp.where(
                    i == 0,
                    FACTORS[k][j],
                    jnp.where(i == 1, FACTORS[k + 2][j], FACTORS[k + 4][j]),
                ).astype(jnp.float32)

            sweep(total, dir_a, dir_b, pick(0, 0), pick(0, 1))
            sweep(total, dir_b, dir_a, pick(1, 0), pick(1, 1))
            return carry

        lax.fori_loop(0, SWEEPS // 2, pair, 0)

    solve(field)
    for x in range(LAYERS):
        for side in range(2):
            value = field[x + 1, side] + dir_a[x + 1, side]
            field[x + 1, side] = value
            start = weight[x, side] * (value - data[x, side]) * inverse[x, side]
            resid[x, side] = start
            dir_a[x + 1, side] = start * (1.0 / CENTER)
            adjoint[x + 1, side] = zeros
    solve(adjoint)

    def around(ref, extra=None):
        def read(layer):
            pair = [ref[here + layer, 0], ref[here + layer, 1]]
            if extra is not None:
                pair = [pair[k] + extra[here + layer, k] for k in range(2)]
            return pair

        below, mine, above = read(0), read(1), read(2)
        return mine, neighbours(mine[0], mine[1], above, below)

    perm_mine, perm_next = around(perm)
    pres_mine, pres_next = around(field)
    adj_mine, adj_next = around(adjoint, dir_a)
    glogk = []
    for side in range(2):
        total = zeros
        for k in range(12):
            other = perm_next[side][k]
            rate = (
                -(adj_mine[side] - adj_next[side][k])
                * (pres_mine[side] - pres_next[side][k])
                * local[k, side]
                / (perm_mine[side] + other)
            )
            total = total + rate * other
        glogk.append(total)

    def apart(even, odd):
        left = left_half()
        return jnp.where(left, even, swap(odd)), jnp.where(left, swap(even), odd)

    first, second = apart(*pres_mine)
    pressure_ref[0] = first
    pressure_ref[1] = second
    first, second = apart(*glogk)
    first, second = first.astype(jnp.bfloat16), second.astype(jnp.bfloat16)
    for m in range(glogk_ref.shape[0]):
        glogk_ref[m, 0] = first
        glogk_ref[m, 1] = second


def physics(own, other, copies):
    f32 = jnp.float32

    def buffer(*lead):
        return pltpu.VMEM((*lead, ROWS, LANES), f32)

    padded = LAYERS + 2
    return pl.pallas_call(
        physics_kernel,
        in_specs=[VMEM] * 2,
        out_specs=[VMEM, VMEM],
        out_shape=[
            jax.ShapeDtypeStruct((2, ROWS, LANES), f32),
            jax.ShapeDtypeStruct((copies, 2, ROWS, LANES), jnp.bfloat16),
        ],
        scratch_shapes=[
            buffer(padded, 2),
            buffer(LAYERS, 12, 2),
            buffer(LAYERS, 2),
            buffer(12, 2),
            buffer(LAYERS, THROWS, 2),
            buffer(LAYERS, 2),
            buffer(LAYERS, 2),
            buffer(LAYERS, 2),
            buffer(padded, 2),
            buffer(padded, 2),
            buffer(padded, 2),
            buffer(padded, 2),
        ],
        compiler_params=pltpu.CompilerParams(vmem_limit_bytes=12 * 2**20),
        cost_estimate=cost(2**32, 2**24),
        name="physics",
    )(own, other)


def gradient_kernel(glogk_ref, basis_ref, out_ref, rows):
    chains = out_ref.shape[0]
    values = glogk_ref[...].astype(jnp.float32).reshape(chains, ROWS, LANES)
    rows[...] = values
    for row in range(ROWS):
        left = rows[:, row, :].astype(jnp.bfloat16)
        part = jnp.dot(
            left,
            basis_ref[row * LANES : (row + 1) * LANES, :],
            preferred_element_type=jnp.float32,
        )
        total = part if row == 0 else total + part
    out_ref[...] = total.astype(jnp.bfloat16)


def gradient_of(glogk, basis):
    chains = glogk.shape[0] * glogk.shape[1]
    return pl.pallas_call(
        gradient_kernel,
        in_specs=[VMEM, VMEM],
        out_specs=VMEM,
        out_shape=jax.ShapeDtypeStruct((chains, basis.shape[1]), jnp.bfloat16),
        scratch_shapes=[pltpu.VMEM((chains, ROWS, LANES), jnp.float32)],
        compiler_params=pltpu.CompilerParams(vmem_limit_bytes=6 * 2**20),
        cost_estimate=cost(2 * chains * basis.size, 2 * basis.size),
        name="gradient",
    )(glogk, basis)


def copies_kernel(one_ref, two_ref, out_ref):
    total = one_ref[...].astype(jnp.float32) + two_ref[...].astype(jnp.float32)
    total = total.astype(jnp.bfloat16)
    for k in range(out_ref.shape[0]):
        out_ref[k] = total


def copies_of(one, two, count):
    return pl.pallas_call(
        copies_kernel,
        in_specs=[VMEM, VMEM],
        out_specs=VMEM,
        out_shape=jax.ShapeDtypeStruct((count, *one.shape), jnp.bfloat16),
        cost_estimate=cost(2**16, 2**19),
        compiler_params=pltpu.CompilerParams(vmem_limit_bytes=4 * 2**20),
        name="copies",
    )(one, two)


def exchange(value, mask, size):
    return lax.ppermute(value, AXES, [(i, i ^ mask) for i in range(size)])


def body(
    theta,
    basis,
    mean_logk,
    face_mult,
    storage,
    sources,
    obs_data,
    obs_weight,
    fault_pairs,
    fault_mult,
    noise,
):
    modes_n, cells_n = lax.axis_size("modes"), lax.axis_size("cells")
    size = cells_n * modes_n

    partial_field = field_of(theta.T, basis).reshape(modes_n, 2, ROWS, LANES)
    parts = lax.all_to_all(partial_field, "modes", 0, 0)
    pieces = combine(
        parts,
        mean_logk.reshape(ROWS, LANES),
        face_mult,
        storage.reshape(ROWS, LANES),
        sources.reshape(ROWS, LANES),
        obs_data.reshape(ROWS, LANES),
        obs_weight.reshape(ROWS, LANES),
        fault_pairs.T,
        fault_mult.reshape(1, SLOT_ROWS * LANES),
    )
    pieces = lax.all_to_all(pieces, "cells", 0, 0)
    others = exchange(pieces, 1, size)
    pressure, glogk = physics(pieces, others, modes_n)
    glogk = lax.all_to_all(glogk, "modes", 0, 0)
    grad_rows = gradient_of(glogk, basis)
    half = cells_n // 2
    grad_rows = copies_of(grad_rows, exchange(grad_rows, half * modes_n, size), half)
    groups = [list(range(half)), list(range(half, cells_n))]
    grad_rows = lax.all_to_all(grad_rows, "cells", 0, 0, axis_index_groups=groups)
    grad = jnp.sum(grad_rows.astype(jnp.float32), 0).T
    theta_next = theta - STEP_SIZE * (grad + theta) + math.sqrt(2.0 * STEP_SIZE) * noise
    return (theta_next, grad, pressure.reshape(2, NY * NZ))


def solution(mesh):
    return jax.shard_map(
        body,
        mesh=mesh,
        in_specs=(
            P("modes", None),
            P("cells", "modes"),
            P("cells"),
            P(None, "cells"),
            P("cells"),
            P("cells"),
            P("cells"),
            P("cells"),
            P("cells", None),
            P("cells"),
            P("modes", None),
        ),
        out_specs=(P("modes", None), P("modes", None), P("modes", "cells")),
        check_vma=False,
    )
```

```python
import math

import jax
import jax.numpy as jnp
from jax import lax
from jax.experimental import pallas as pl
from jax.experimental.pallas import tpu as pltpu
from jax.sharding import PartitionSpec as P

NY = 32
NZ = 64
SWEEPS = 6
LAYERS = 16
LANES = 128
ROWS = NY * NZ // LANES
SLOT_ROWS = 2
PIECE = 48
THROWS = 3

LOW_EIG = 0.1
HIGH_EIG = 1.9
STEP_SIZE = 0.01
AXES = ("cells", "modes")
VMEM = pl.BlockSpec(memory_space=pltpu.VMEM)


def place():
    return lax.axis_index("cells"), lax.axis_index("modes") & 1


def cost(flops, bytes_accessed):
    return pl.CostEstimate(flops=flops, bytes_accessed=bytes_accessed, transcendentals=0)


def chebyshev():
    center = 0.5 * (HIGH_EIG + LOW_EIG)
    half = 0.5 * (HIGH_EIG - LOW_EIG)
    sigma = center / half
    rho = 1.0 / sigma
    factors = []
    for _ in range(SWEEPS):
        rho_next = 1.0 / (2.0 * sigma - rho)
        factors.append((rho_next * rho, 2.0 * rho_next / half))
        rho = rho_next
    return center, factors


CENTER, FACTORS = chebyshev()


def field_kernel(theta_hbm, basis_hbm, out_ref, theta, basis, sems):
    steps = sems.shape[0] - 1
    count = basis.shape[0] // steps
    copies = [pltpu.make_async_copy(theta_hbm, theta, sems.at[steps])]
    for step in range(steps):
        rows = pl.ds(step * count, count)
        copies.append(pltpu.make_async_copy(basis_hbm.at[rows], basis.at[rows], sems.at[step]))
    for copy in copies:
        copy.start()
    copies[0].wait()
    theta_b = theta[...].astype(jnp.bfloat16)
    for step in range(steps):
        copies[step + 1].wait()
        part = lax.dot_general(
            theta_b,
            basis[step * count : (step + 1) * count, :],
            (((1,), (1,)), ((), ())),
            preferred_element_type=jnp.float32,
        )
        for row in range(count // LANES):
            out_ref[:, step * (count // LANES) + row, :] = part[:, row * LANES : (row + 1) * LANES]


def field_of(theta, basis):
    chains, modes = theta.shape
    steps = 2
    return pl.pallas_call(
        field_kernel,
        in_specs=[pl.BlockSpec(memory_space=pltpu.HBM)] * 2,
        out_specs=VMEM,
        out_shape=jax.ShapeDtypeStruct((chains, ROWS, LANES), jnp.float32),
        scratch_shapes=[
            pltpu.VMEM(theta.shape, theta.dtype),
            pltpu.VMEM(basis.shape, basis.dtype),
            pltpu.SemaphoreType.DMA((steps + 1,)),
        ],
        cost_estimate=cost(2 * chains * modes * ROWS * LANES, 2 * modes * ROWS * LANES),
        compiler_params=pltpu.CompilerParams(vmem_limit_bytes=8 * 2**20),
        name="field",
    )(
        pltpu.with_memory_space_constraint(theta, pltpu.HBM),
        pltpu.with_memory_space_constraint(basis, pltpu.HBM),
    )


def left_half():
    return lax.broadcasted_iota(jnp.int32, (ROWS, LANES), 1) < NZ


def swap(a):
    return pltpu.roll(a, NZ, 1)


def span(low, high):
    return low, (high - low) / 65535.0


MULT_SPAN, STORE_SPAN, WELL_SPAN, UNIT_SPAN = (
    span(0.3, 3.0),
    span(0.05, 0.5),
    span(-6.0, 6.0),
    span(0.1, 1.0),
)


def code16(a, within):
    low, step = within
    return ((a - low) * (1.0 / step) + 0.5).astype(jnp.int32) - 32768


def value16(code, within):
    low, step = within
    return (code + 32768).astype(jnp.float32) * step + low


def pack(high, low):
    return (high << 16) | (low & 0xFFFF)


def high16(word):
    return word >> 16


def low16(word):
    return (word << 16) >> 16


def combine_kernel(
    parts_ref,
    mean_ref,
    face_ref,
    storage_ref,
    sources_ref,
    data_ref,
    weight_ref,
    pairs_ref,
    fault_ref,
    out_ref,
):
    total = jnp.sum(parts_ref[...], axis=0)
    mean = mean_ref[...]
    first, second = total[0] + mean, total[1] + mean
    left = left_half()
    even = jnp.where(left, first, swap(second))
    odd = jnp.where(left, swap(first), second)
    top = jnp.max(jnp.maximum(jnp.abs(even), jnp.abs(odd)), axis=(0, 1), keepdims=True)
    bound = (top * 256.0).astype(jnp.int32) + 1
    factor = (32767.0 * 256.0) / bound.astype(jnp.float32)

    def scaled(a):
        return jnp.floor(a * factor + 0.5).astype(jnp.int32)

    def rows_of(a):
        return jnp.concatenate(
            [a[:, row * LANES : (row + 1) * LANES] for row in range(a.shape[1] // LANES)], 0
        )

    face = face_ref[...]
    mult = [code16(rows_of(face[k : k + 1]), MULT_SPAN) for k in range(3)]
    store = code16(storage_ref[...], STORE_SPAN)
    source = code16(sources_ref[...], WELL_SPAN)
    data = code16(data_ref[...], WELL_SPAN)
    weight = code16(weight_ref[...], UNIT_SPAN)
    near, far = rows_of(pairs_ref[0:1]), rows_of(pairs_ref[1:2])
    code = near * 4 + jnp.where(near == far, 0, far - near - NZ)
    fault = (rows_of(fault_ref[...]) * 65535.0 + 0.5).astype(jnp.int32) - 32768
    bounds = jnp.broadcast_to(bound, (2, LANES))
    zeros = jnp.zeros((2, LANES), jnp.int32)
    forms = (
        [
            pack(mult[0], mult[1]),
            pack(mult[2][0:8], mult[2][8:16]),
            pack(store[0:4], store[4:8]),
            zeros,
            bounds,
        ],
        [
            pack(source, data),
            pack(weight[0:8], weight[8:16]),
            pack(store[8:12], store[12:16]),
            pack(code, fault),
            bounds,
        ],
    )
    forms = [jnp.concatenate(form, 0) for form in forms]
    fixed = jnp.where(place()[1] == 0, forms[0], forms[1])
    field = pack(scaled(even), scaled(odd))
    for k in range(out_ref.shape[0]):
        out_ref[k, 0:ROWS] = field
        out_ref[k, ROWS:PIECE] = fixed


def combine(parts, *fixed):
    return pl.pallas_call(
        combine_kernel,
        in_specs=[VMEM] * (1 + len(fixed)),
        out_specs=VMEM,
        out_shape=jax.ShapeDtypeStruct((LAYERS, PIECE, LANES), jnp.int32),
        cost_estimate=cost(2**17, 2**20),
        compiler_params=pltpu.CompilerParams(vmem_limit_bytes=4 * 2**20),
        name="combine",
    )(parts, *fixed)


def harmonic(left, right):
    return 2.0 * left * right / (left + right)


def ahead(a, s):
    return pltpu.roll(a, LANES - s, 1)


def behind(a, s):
    return pltpu.roll(a, s, 1)


def up(a):
    return pltpu.roll(a, ROWS - 1, 0)


def down(a):
    return pltpu.roll(a, 1, 0)


def spread(a):
    left, other = left_half(), swap(a)
    return jnp.where(left, a, other), jnp.where(left, other, a)


def neighbours(even, odd, above, below):
    to_even = [above[0], below[0], ahead(even, 1), behind(even, 1), odd, down(odd)]
    to_odd = [above[1], below[1], ahead(odd, 1), behind(odd, 1), up(even), even]
    for s in range(1, THROWS + 1):
        to_even.append(ahead(odd, s))
        to_odd.append(up(ahead(even, s)))
    for s in range(1, THROWS + 1):
        to_even.append(down(behind(odd, s)))
        to_odd.append(behind(even, s))
    return to_even, to_odd


def physics_kernel(
    own_ref,
    other_ref,
    pressure_ref,
    glogk_ref,
    perm,
    coef,
    inverse,
    local,
    fault,
    weight,
    data,
    resid,
    field,
    adjoint,
    dir_a,
    dir_b,
):
    here, core = place()
    zeros = jnp.zeros((ROWS, LANES), jnp.float32)
    for pad in (0, LAYERS + 1):
        for k in range(2):
            perm[pad, k] = zeros + 1.0
            field[pad, k] = zeros
            adjoint[pad, k] = zeros
            dir_a[pad, k] = zeros
            dir_b[pad, k] = zeros
    for x in range(LAYERS):
        word = own_ref[x, 0:ROWS]
        factor = own_ref[x, PIECE - 1 : PIECE].astype(jnp.float32) * (1.0 / (32767.0 * 256.0))
        perm[x + 1, 0] = jnp.exp(high16(word).astype(jnp.float32) * factor)
        perm[x + 1, 1] = jnp.exp(low16(word).astype(jnp.float32) * factor)

    lane = lax.broadcasted_iota(jnp.int32, (ROWS, LANES), 1)
    row = lax.broadcasted_iota(jnp.int32, (ROWS, LANES), 0)
    z_inside = (lane & (NZ - 1)) < NZ - 1
    y_inside = row < ROWS - 1
    keys = lax.broadcasted_iota(jnp.int32, (THROWS * ROWS, SLOT_ROWS * LANES), 0)
    lanes_of = lax.broadcasted_iota(jnp.int32, (LANES, SLOT_ROWS * LANES), 0)

    def join(x):
        own, other = own_ref[x, PIECE - 4 : PIECE - 2], other_ref[x, PIECE - 4 : PIECE - 2]
        slots = jnp.where(core == 0, other, own)
        slots = jnp.concatenate([slots[h : h + 1] for h in range(SLOT_ROWS)], 1)
        code, amount = high16(slots), low16(slots) + 32768
        throw, cell = code & 3, code >> 2
        key = jnp.where(throw > 0, (throw - 1) * ROWS + (cell >> 7), -1)
        hit = keys == key
        parts = [
            jnp.where(hit, part.astype(jnp.float32), 0.0) for part in (amount >> 8, amount & 255)
        ]
        rows_hot = jnp.concatenate(parts, 0).astype(jnp.bfloat16)
        lanes_hot = jnp.where(lanes_of == (cell & (LANES - 1)), 1.0, 0.0).astype(jnp.bfloat16)
        sums = lax.dot_general(
            rows_hot, lanes_hot, (((1,), (1,)), ((), ())), preferred_element_type=jnp.float32
        )
        count = THROWS * ROWS
        total = (sums[:count] * 256.0 + sums[count:]) * (1.0 / 65535.0)
        for s in range(THROWS):
            even, odd = spread(total[s * ROWS : (s + 1) * ROWS])
            fault[x, s, 0] = even
            fault[x, s, 1] = odd

    for x in range(LAYERS):
        join(x)

    def prepare(x, carry):
        own, other = own_ref[x, ROWS:PIECE], other_ref[x, ROWS:PIECE]
        first = jnp.where(core == 0, own, other)
        second = jnp.where(core == 0, other, own)
        mult_x = spread(value16(high16(first[0:16]), MULT_SPAN))
        mult_y = spread(value16(low16(first[0:16]), MULT_SPAN))
        halves = (high16(first[16:24]), low16(first[16:24]))
        mult_z = spread(value16(jnp.concatenate(halves, 0), MULT_SPAN))
        store = [op(w[24:28]) for w in (first, second) for op in (high16, low16)]
        storage = spread(value16(jnp.concatenate(store, 0), STORE_SPAN))
        source = spread(value16(high16(second[0:16]), WELL_SPAN))
        obs_data = spread(value16(low16(second[0:16]), WELL_SPAN))
        halves = (high16(second[16:24]), low16(second[16:24]))
        obs_weight = spread(value16(jnp.concatenate(halves, 0), UNIT_SPAN))
        even, odd = perm[x + 1, 0], perm[x + 1, 1]
        inside = jnp.where(x < LAYERS - 1, 1.0, 0.0)
        xp_even = harmonic(even, perm[x + 2, 0]) * mult_x[0] * inside
        xp_odd = harmonic(odd, perm[x + 2, 1]) * mult_x[1] * inside
        xm_even, xm_odd = carry
        zp_even = jnp.where(z_inside, harmonic(even, ahead(even, 1)) * mult_z[0], 0.0)
        zp_odd = jnp.where(z_inside, harmonic(odd, ahead(odd, 1)) * mult_z[1], 0.0)
        y_even = harmonic(even, odd) * mult_y[0]
        y_odd = jnp.where(y_inside, harmonic(odd, up(even)) * mult_y[1], 0.0)
        to_even = [xp_even, xm_even, zp_even, behind(zp_even, 1), y_even, down(y_odd)]
        to_odd = [xp_odd, xm_odd, zp_odd, behind(zp_odd, 1), y_odd, y_even]
        back_even, back_odd = [], []
        for s in range(1, THROWS + 1):
            fault_even = harmonic(even, ahead(odd, s)) * fault[x, s - 1, 0]
            fault_odd = harmonic(odd, up(ahead(even, s))) * fault[x, s - 1, 1]
            to_even.append(fault_even)
            to_odd.append(fault_odd)
            back_even.append(down(behind(fault_odd, s)))
            back_odd.append(behind(fault_even, s))
        to_even += back_even
        to_odd += back_odd

        @pl.when(x == here)
        def _():
            for k in range(12):
                local[k, 0] = to_even[k]
                local[k, 1] = to_odd[k]

        for side, trans in ((0, to_even), (1, to_odd)):
            diag = storage[side]
            for t in trans:
                diag = diag + t
            inv = 1.0 / diag
            inverse[x, side] = inv
            for k in range(12):
                value = trans[k] * inv
                if side == 0 and k in (5, 9, 10, 11):
                    value = up(value)
                if side == 1 and k in (4, 6, 7, 8):
                    value = down(value)
                coef[x, k, side] = value
            weight[x, side] = obs_weight[side]
            data[x, side] = obs_data[side]
            start = source[side] * inv
            resid[x, side] = start
            dir_a[x + 1, side] = start * (1.0 / CENTER)
            field[x + 1, side] = zeros
        return xp_even, xp_odd

    lax.fori_loop(0, LAYERS, prepare, (zeros, zeros), unroll=4)

    def sweep(total, source_dir, target_dir, keep, gain, base=0, count=LAYERS):
        for step in range(count):
            x = base + step
            even, odd = source_dir[x + 1, 0], source_dir[x + 1, 1]
            c = lambda k, side: coef[x, k, side]
            acc_even = c(0, 0) * source_dir[x + 2, 0] + c(1, 0) * source_dir[x, 0]
            acc_odd = c(0, 1) * source_dir[x + 2, 1] + c(1, 1) * source_dir[x, 1]
            acc_even += c(4, 0) * odd
            acc_odd += c(5, 1) * even
            low = c(5, 0) * odd
            high = c(4, 1) * even
            for s in range(1, THROWS + 1):
                even_ahead, odd_ahead = ahead(even, s), ahead(odd, s)
                even_behind, odd_behind = behind(even, s), behind(odd, s)
                if s == 1:
                    acc_even += c(2, 0) * even_ahead + c(3, 0) * even_behind
                    acc_odd += c(2, 1) * odd_ahead + c(3, 1) * odd_behind
                acc_even += c(5 + s, 0) * odd_ahead
                acc_odd += c(8 + s, 1) * even_behind
                low += c(8 + s, 0) * odd_behind
                high += c(5 + s, 1) * even_ahead
            acc_even += down(low)
            acc_odd += up(high)
            for side, own, acc in ((0, even, acc_even), (1, odd, acc_odd)):
                left = resid[x, side] - (own - acc)
                resid[x, side] = left
                total[x + 1, side] = total[x + 1, side] + own
                target_dir[x + 1, side] = keep * own + gain * left

    def solve(total):
        def pair(i, carry):
            def pick(k, j):
                return jnp.where(
                    i == 0,
                    FACTORS[k][j],
                    jnp.where(i == 1, FACTORS[k + 2][j], FACTORS[k + 4][j]),
                ).astype(jnp.float32)

            sweep(total, dir_a, dir_b, pick(0, 0), pick(0, 1))
            sweep(total, dir_b, dir_a, pick(1, 0), pick(1, 1))
            return carry

        lax.fori_loop(0, SWEEPS // 2, pair, 0)

    solve(field)
    for x in range(LAYERS):
        for side in range(2):
            value = field[x + 1, side] + dir_a[x + 1, side]
            field[x + 1, side] = value
            start = weight[x, side] * (value - data[x, side]) * inverse[x, side]
            resid[x, side] = start
            dir_a[x + 1, side] = start * (1.0 / CENTER)
            adjoint[x + 1, side] = zeros
    for k in range(SWEEPS):
        reach = SWEEPS - k
        count = min(2 * reach + 1, LAYERS)
        base = jnp.clip(here - reach, 0, LAYERS - count)
        pair = (dir_a, dir_b) if k % 2 == 0 else (dir_b, dir_a)
        sweep(adjoint, *pair, *FACTORS[k], base, count)

    def around(ref, extra=None):
        def read(layer):
            pair = [ref[here + layer, 0], ref[here + layer, 1]]
            if extra is not None:
                pair = [pair[k] + extra[here + layer, k] for k in range(2)]
            return pair

        below, mine, above = read(0), read(1), read(2)
        return mine, neighbours(mine[0], mine[1], above, below)

    perm_mine, perm_next = around(perm)
    pres_mine, pres_next = around(field)
    adj_mine, adj_next = around(adjoint, dir_a)
    glogk = []
    for side in range(2):
        total = zeros
        for k in range(12):
            other = perm_next[side][k]
            rate = (
                -(adj_mine[side] - adj_next[side][k])
                * (pres_mine[side] - pres_next[side][k])
                * local[k, side]
                / (perm_mine[side] + other)
            )
            total = total + rate * other
        glogk.append(total)

    def apart(even, odd):
        left = left_half()
        return jnp.where(left, even, swap(odd)), jnp.where(left, swap(even), odd)

    first, second = apart(*pres_mine)
    pressure_ref[0] = first
    pressure_ref[1] = second
    first, second = apart(*glogk)
    first, second = first.astype(jnp.bfloat16), second.astype(jnp.bfloat16)
    for m in range(glogk_ref.shape[0]):
        glogk_ref[m, 0] = first
        glogk_ref[m, 1] = second


def physics(own, other, copies):
    f32 = jnp.float32

    def buffer(*lead):
        return pltpu.VMEM((*lead, ROWS, LANES), f32)

    padded = LAYERS + 2
    return pl.pallas_call(
        physics_kernel,
        in_specs=[VMEM] * 2,
        out_specs=[VMEM, VMEM],
        out_shape=[
            jax.ShapeDtypeStruct((2, ROWS, LANES), f32),
            jax.ShapeDtypeStruct((copies, 2, ROWS, LANES), jnp.bfloat16),
        ],
        scratch_shapes=[
            buffer(padded, 2),
            buffer(LAYERS, 12, 2),
            buffer(LAYERS, 2),
            buffer(12, 2),
            buffer(LAYERS, THROWS, 2),
            buffer(LAYERS, 2),
            buffer(LAYERS, 2),
            buffer(LAYERS, 2),
            buffer(padded, 2),
            buffer(padded, 2),
            buffer(padded, 2),
            buffer(padded, 2),
        ],
        compiler_params=pltpu.CompilerParams(vmem_limit_bytes=12 * 2**20),
        cost_estimate=cost(2**32, 2**24),
        name="physics",
    )(own, other)


def gradient_kernel(glogk_ref, basis_ref, out_ref, rows):
    chains = out_ref.shape[0]
    values = glogk_ref[...].astype(jnp.float32).reshape(chains, ROWS, LANES)
    rows[...] = values
    for row in range(ROWS):
        left = rows[:, row, :].astype(jnp.bfloat16)
        part = jnp.dot(
            left,
            basis_ref[row * LANES : (row + 1) * LANES, :],
            preferred_element_type=jnp.float32,
        )
        total = part if row == 0 else total + part
    out_ref[...] = total.astype(jnp.bfloat16)


def gradient_of(glogk, basis):
    chains = glogk.shape[0] * glogk.shape[1]
    return pl.pallas_call(
        gradient_kernel,
        in_specs=[VMEM, VMEM],
        out_specs=VMEM,
        out_shape=jax.ShapeDtypeStruct((chains, basis.shape[1]), jnp.bfloat16),
        scratch_shapes=[pltpu.VMEM((chains, ROWS, LANES), jnp.float32)],
        compiler_params=pltpu.CompilerParams(vmem_limit_bytes=6 * 2**20),
        cost_estimate=cost(2 * chains * basis.size, 2 * basis.size),
        name="gradient",
    )(glogk, basis)


def copies_kernel(one_ref, two_ref, out_ref):
    total = one_ref[...].astype(jnp.float32) + two_ref[...].astype(jnp.float32)
    total = total.astype(jnp.bfloat16)
    for k in range(out_ref.shape[0]):
        out_ref[k] = total


def copies_of(one, two, count):
    return pl.pallas_call(
        copies_kernel,
        in_specs=[VMEM, VMEM],
        out_specs=VMEM,
        out_shape=jax.ShapeDtypeStruct((count, *one.shape), jnp.bfloat16),
        cost_estimate=cost(2**16, 2**19),
        compiler_params=pltpu.CompilerParams(vmem_limit_bytes=4 * 2**20),
        name="copies",
    )(one, two)


def exchange(value, mask, size):
    return lax.ppermute(value, AXES, [(i, i ^ mask) for i in range(size)])


def body(
    theta,
    basis,
    mean_logk,
    face_mult,
    storage,
    sources,
    obs_data,
    obs_weight,
    fault_pairs,
    fault_mult,
    noise,
):
    modes_n, cells_n = lax.axis_size("modes"), lax.axis_size("cells")
    size = cells_n * modes_n

    partial_field = field_of(theta.T, basis).reshape(modes_n, 2, ROWS, LANES)
    parts = lax.all_to_all(partial_field, "modes", 0, 0)
    pieces = combine(
        parts,
        mean_logk.reshape(ROWS, LANES),
        face_mult,
        storage.reshape(ROWS, LANES),
        sources.reshape(ROWS, LANES),
        obs_data.reshape(ROWS, LANES),
        obs_weight.reshape(ROWS, LANES),
        fault_pairs.T,
        fault_mult.reshape(1, SLOT_ROWS * LANES),
    )
    pieces = lax.all_to_all(pieces, "cells", 0, 0)
    others = exchange(pieces, 1, size)
    pressure, glogk = physics(pieces, others, modes_n)
    glogk = lax.all_to_all(glogk, "modes", 0, 0)
    grad_rows = gradient_of(glogk, basis)
    half = cells_n // 2
    grad_rows = copies_of(grad_rows, exchange(grad_rows, half * modes_n, size), half)
    groups = [list(range(half)), list(range(half, cells_n))]
    grad_rows = lax.all_to_all(grad_rows, "cells", 0, 0, axis_index_groups=groups)
    grad = jnp.sum(grad_rows.astype(jnp.float32), 0).T
    theta_next = theta - STEP_SIZE * (grad + theta) + math.sqrt(2.0 * STEP_SIZE) * noise
    return (theta_next, grad, pressure.reshape(2, NY * NZ))


def solution(mesh):
    return jax.shard_map(
        body,
        mesh=mesh,
        in_specs=(
            P("modes", None),
            P("cells", "modes"),
            P("cells"),
            P(None, "cells"),
            P("cells"),
            P("cells"),
            P("cells"),
            P("cells"),
            P("cells", None),
            P("cells"),
            P("modes", None),
        ),
        out_specs=(P("modes", None), P("modes", None), P("modes", "cells")),
        check_vma=False,
    )
```

```python
import math

import jax
import jax.numpy as jnp
from jax import lax
from jax.experimental import pallas as pl
from jax.experimental.pallas import tpu as pltpu
from jax.sharding import PartitionSpec as P

NY = 32
NZ = 64
SWEEPS = 6
LAYERS = 16
LANES = 128
ROWS = NY * NZ // LANES
SLOT_ROWS = 2
PIECE = 48
THROWS = 3

LOW_EIG = 0.1
HIGH_EIG = 1.9
STEP_SIZE = 0.01
AXES = ("cells", "modes")
VMEM = pl.BlockSpec(memory_space=pltpu.VMEM)


def place():
    return lax.axis_index("cells"), lax.axis_index("modes") & 1


def turn(mode):
    return 4 * (mode & 1) + 2 * (mode >> 1)


def cost(flops, bytes_accessed):
    return pl.CostEstimate(flops=flops, bytes_accessed=bytes_accessed, transcendentals=0)


def chebyshev():
    center = 0.5 * (HIGH_EIG + LOW_EIG)
    half = 0.5 * (HIGH_EIG - LOW_EIG)
    sigma = center / half
    rho = 1.0 / sigma
    factors = []
    for _ in range(SWEEPS):
        rho_next = 1.0 / (2.0 * sigma - rho)
        factors.append((rho_next * rho, 2.0 * rho_next / half))
        rho = rho_next
    return center, factors


CENTER, FACTORS = chebyshev()


def field_kernel(theta_hbm, basis_hbm, out_ref, theta, basis, sems):
    steps = sems.shape[0] - 1
    count = basis.shape[0] // steps
    copies = [pltpu.make_async_copy(theta_hbm, theta, sems.at[steps])]
    for step in range(steps):
        rows = pl.ds(step * count, count)
        copies.append(pltpu.make_async_copy(basis_hbm.at[rows], basis.at[rows], sems.at[step]))
    for copy in copies:
        copy.start()
    copies[0].wait()
    theta_b = theta[...].astype(jnp.bfloat16)
    for step in range(steps):
        copies[step + 1].wait()
        part = lax.dot_general(
            theta_b,
            basis[step * count : (step + 1) * count, :],
            (((1,), (1,)), ((), ())),
            preferred_element_type=jnp.float32,
        )
        for row in range(count // LANES):
            out_ref[:, step * (count // LANES) + row, :] = part[:, row * LANES : (row + 1) * LANES]


def field_of(theta, basis):
    chains, modes = theta.shape
    steps = 2
    return pl.pallas_call(
        field_kernel,
        in_specs=[pl.BlockSpec(memory_space=pltpu.HBM)] * 2,
        out_specs=VMEM,
        out_shape=jax.ShapeDtypeStruct((chains, ROWS, LANES), jnp.float32),
        scratch_shapes=[
            pltpu.VMEM(theta.shape, theta.dtype),
            pltpu.VMEM(basis.shape, basis.dtype),
            pltpu.SemaphoreType.DMA((steps + 1,)),
        ],
        cost_estimate=cost(2 * chains * modes * ROWS * LANES, 2 * modes * ROWS * LANES),
        compiler_params=pltpu.CompilerParams(vmem_limit_bytes=8 * 2**20),
        name="field",
    )(
        pltpu.with_memory_space_constraint(theta, pltpu.HBM),
        pltpu.with_memory_space_constraint(basis, pltpu.HBM),
    )


def left_half():
    return lax.broadcasted_iota(jnp.int32, (ROWS, LANES), 1) < NZ


def swap(a):
    return pltpu.roll(a, NZ, 1)


def span(low, high):
    return low, (high - low) / 65535.0


MULT_SPAN, STORE_SPAN, WELL_SPAN, UNIT_SPAN = (
    span(0.3, 3.0),
    span(0.05, 0.5),
    span(-6.0, 6.0),
    span(0.1, 1.0),
)


def code16(a, within):
    low, step = within
    return ((a - low) * (1.0 / step) + 0.5).astype(jnp.int32) - 32768


def value16(code, within):
    low, step = within
    return (code + 32768).astype(jnp.float32) * step + low


def pack(high, low):
    return (high << 16) | (low & 0xFFFF)


def high16(word):
    return word >> 16


def low16(word):
    return (word << 16) >> 16


def combine_kernel(
    parts_ref,
    mean_ref,
    face_ref,
    storage_ref,
    sources_ref,
    data_ref,
    weight_ref,
    pairs_ref,
    fault_ref,
    out_ref,
):
    total = jnp.sum(parts_ref[...], axis=0)
    mean = mean_ref[...]
    first, second = total[0] + mean, total[1] + mean
    left = left_half()
    even = jnp.where(left, first, swap(second))
    odd = jnp.where(left, swap(first), second)
    top = jnp.max(jnp.maximum(jnp.abs(even), jnp.abs(odd)), axis=(0, 1), keepdims=True)
    bound = (top * 256.0).astype(jnp.int32) + 1
    factor = (32767.0 * 256.0) / bound.astype(jnp.float32)

    def scaled(a):
        return jnp.floor(a * factor + 0.5).astype(jnp.int32)

    def rows_of(a):
        return jnp.concatenate(
            [a[:, row * LANES : (row + 1) * LANES] for row in range(a.shape[1] // LANES)], 0
        )

    face = face_ref[...]
    mult = [code16(rows_of(face[k : k + 1]), MULT_SPAN) for k in range(3)]
    store = code16(storage_ref[...], STORE_SPAN)
    source = code16(sources_ref[...], WELL_SPAN)
    data = code16(data_ref[...], WELL_SPAN)
    weight = code16(weight_ref[...], UNIT_SPAN)
    near, far = rows_of(pairs_ref[0:1]), rows_of(pairs_ref[1:2])
    code = near * 4 + jnp.where(near == far, 0, far - near - NZ)
    fault = (rows_of(fault_ref[...]) * 65535.0 + 0.5).astype(jnp.int32) - 32768
    bounds = jnp.broadcast_to(bound, (2, LANES))
    zeros = jnp.zeros((2, LANES), jnp.int32)
    forms = (
        [
            pack(mult[0], mult[1]),
            pack(mult[2][0:8], mult[2][8:16]),
            pack(store[0:4], store[4:8]),
            zeros,
            bounds,
        ],
        [
            pack(source, data),
            pack(weight[0:8], weight[8:16]),
            pack(store[8:12], store[12:16]),
            pack(code, fault),
            bounds,
        ],
    )
    forms = [jnp.concatenate(form, 0) for form in forms]
    fixed = jnp.where(place()[1] == 0, forms[0], forms[1])
    field = pack(scaled(even), scaled(odd))
    for k in range(out_ref.shape[0]):
        out_ref[k, 0:ROWS] = field
        out_ref[k, ROWS:PIECE] = fixed


def combine(parts, *fixed):
    return pl.pallas_call(
        combine_kernel,
        in_specs=[VMEM] * (1 + len(fixed)),
        out_specs=VMEM,
        out_shape=jax.ShapeDtypeStruct((LAYERS, PIECE, LANES), jnp.int32),
        cost_estimate=cost(2**17, 2**20),
        compiler_params=pltpu.CompilerParams(vmem_limit_bytes=4 * 2**20),
        name="combine",
    )(parts, *fixed)


def harmonic(left, right):
    return 2.0 * left * right / (left + right)


def ahead(a, s):
    return pltpu.roll(a, LANES - s, 1)


def behind(a, s):
    return pltpu.roll(a, s, 1)


def up(a):
    return pltpu.roll(a, ROWS - 1, 0)


def down(a):
    return pltpu.roll(a, 1, 0)


def spread(a):
    left, other = left_half(), swap(a)
    return jnp.where(left, a, other), jnp.where(left, other, a)


def neighbours(even, odd, above, below):
    to_even = [above[0], below[0], ahead(even, 1), behind(even, 1), odd, down(odd)]
    to_odd = [above[1], below[1], ahead(odd, 1), behind(odd, 1), up(even), even]
    for s in range(1, THROWS + 1):
        to_even.append(ahead(odd, s))
        to_odd.append(up(ahead(even, s)))
    for s in range(1, THROWS + 1):
        to_even.append(down(behind(odd, s)))
        to_odd.append(behind(even, s))
    return to_even, to_odd


def physics_kernel(
    own_ref,
    other_ref,
    pressure_ref,
    glogk_ref,
    perm,
    coef,
    inverse,
    local,
    fault,
    weight,
    data,
    resid,
    field,
    adjoint,
    dir_a,
    dir_b,
):
    here, core = place()
    mode = lax.axis_index("modes")
    own_turn, other_turn = turn(mode), turn(mode ^ 1)

    def own_at(x):
        return (x - own_turn) & (LAYERS - 1)

    def other_at(x):
        return (x - other_turn) & (LAYERS - 1)

    zeros = jnp.zeros((ROWS, LANES), jnp.float32)
    for pad in (0, LAYERS + 1):
        for k in range(2):
            perm[pad, k] = zeros + 1.0
            field[pad, k] = zeros
            adjoint[pad, k] = zeros
            dir_a[pad, k] = zeros
            dir_b[pad, k] = zeros
    for x in range(LAYERS):
        word = own_ref[own_at(x), 0:ROWS]
        factor = own_ref[own_at(x), PIECE - 1 : PIECE].astype(jnp.float32) * (1.0 / (32767.0 * 256.0))
        perm[x + 1, 0] = jnp.exp(high16(word).astype(jnp.float32) * factor)
        perm[x + 1, 1] = jnp.exp(low16(word).astype(jnp.float32) * factor)

    lane = lax.broadcasted_iota(jnp.int32, (ROWS, LANES), 1)
    row = lax.broadcasted_iota(jnp.int32, (ROWS, LANES), 0)
    z_inside = (lane & (NZ - 1)) < NZ - 1
    y_inside = row < ROWS - 1
    keys = lax.broadcasted_iota(jnp.int32, (THROWS * ROWS, SLOT_ROWS * LANES), 0)
    lanes_of = lax.broadcasted_iota(jnp.int32, (LANES, SLOT_ROWS * LANES), 0)

    def join(x):
        own = own_ref[own_at(x), PIECE - 4 : PIECE - 2]
        other = other_ref[other_at(x), PIECE - 4 : PIECE - 2]
        slots = jnp.where(core == 0, other, own)
        slots = jnp.concatenate([slots[h : h + 1] for h in range(SLOT_ROWS)], 1)
        code, amount = high16(slots), low16(slots) + 32768
        throw, cell = code & 3, code >> 2
        key = jnp.where(throw > 0, (throw - 1) * ROWS + (cell >> 7), -1)
        hit = keys == key
        parts = [
            jnp.where(hit, part.astype(jnp.float32), 0.0) for part in (amount >> 8, amount & 255)
        ]
        rows_hot = jnp.concatenate(parts, 0).astype(jnp.bfloat16)
        lanes_hot = jnp.where(lanes_of == (cell & (LANES - 1)), 1.0, 0.0).astype(jnp.bfloat16)
        sums = lax.dot_general(
            rows_hot, lanes_hot, (((1,), (1,)), ((), ())), preferred_element_type=jnp.float32
        )
        count = THROWS * ROWS
        total = (sums[:count] * 256.0 + sums[count:]) * (1.0 / 65535.0)
        for s in range(THROWS):
            even, odd = spread(total[s * ROWS : (s + 1) * ROWS])
            fault[x, s, 0] = even
            fault[x, s, 1] = odd

    for x in range(LAYERS):
        join(x)

    def prepare(x, carry):
        own, other = own_ref[own_at(x), ROWS:PIECE], other_ref[other_at(x), ROWS:PIECE]
        first = jnp.where(core == 0, own, other)
        second = jnp.where(core == 0, other, own)
        mult_x = spread(value16(high16(first[0:16]), MULT_SPAN))
        mult_y = spread(value16(low16(first[0:16]), MULT_SPAN))
        halves = (high16(first[16:24]), low16(first[16:24]))
        mult_z = spread(value16(jnp.concatenate(halves, 0), MULT_SPAN))
        store = [op(w[24:28]) for w in (first, second) for op in (high16, low16)]
        storage = spread(value16(jnp.concatenate(store, 0), STORE_SPAN))
        source = spread(value16(high16(second[0:16]), WELL_SPAN))
        obs_data = spread(value16(low16(second[0:16]), WELL_SPAN))
        halves = (high16(second[16:24]), low16(second[16:24]))
        obs_weight = spread(value16(jnp.concatenate(halves, 0), UNIT_SPAN))
        even, odd = perm[x + 1, 0], perm[x + 1, 1]
        inside = jnp.where(x < LAYERS - 1, 1.0, 0.0)
        xp_even = harmonic(even, perm[x + 2, 0]) * mult_x[0] * inside
        xp_odd = harmonic(odd, perm[x + 2, 1]) * mult_x[1] * inside
        xm_even, xm_odd = carry
        zp_even = jnp.where(z_inside, harmonic(even, ahead(even, 1)) * mult_z[0], 0.0)
        zp_odd = jnp.where(z_inside, harmonic(odd, ahead(odd, 1)) * mult_z[1], 0.0)
        y_even = harmonic(even, odd) * mult_y[0]
        y_odd = jnp.where(y_inside, harmonic(odd, up(even)) * mult_y[1], 0.0)
        to_even = [xp_even, xm_even, zp_even, behind(zp_even, 1), y_even, down(y_odd)]
        to_odd = [xp_odd, xm_odd, zp_odd, behind(zp_odd, 1), y_odd, y_even]
        back_even, back_odd = [], []
        for s in range(1, THROWS + 1):
            fault_even = harmonic(even, ahead(odd, s)) * fault[x, s - 1, 0]
            fault_odd = harmonic(odd, up(ahead(even, s))) * fault[x, s - 1, 1]
            to_even.append(fault_even)
            to_odd.append(fault_odd)
            back_even.append(down(behind(fault_odd, s)))
            back_odd.append(behind(fault_even, s))
        to_even += back_even
        to_odd += back_odd

        @pl.when(x == here)
        def _():
            for k in range(12):
                local[k, 0] = to_even[k]
                local[k, 1] = to_odd[k]

        for side, trans in ((0, to_even), (1, to_odd)):
            diag = storage[side]
            for t in trans:
                diag = diag + t
            inv = 1.0 / diag
            inverse[x, side] = inv
            for k in range(12):
                value = trans[k] * inv
                if side == 0 and k in (5, 9, 10, 11):
                    value = up(value)
                if side == 1 and k in (4, 6, 7, 8):
                    value = down(value)
                coef[x, k, side] = value
            weight[x, side] = obs_weight[side]
            data[x, side] = obs_data[side]
            start = source[side] * inv
            resid[x, side] = start
            dir_a[x + 1, side] = start * (1.0 / CENTER)
            field[x + 1, side] = zeros
        return xp_even, xp_odd

    lax.fori_loop(0, LAYERS, prepare, (zeros, zeros), unroll=4)

    def sweep(total, source_dir, target_dir, keep, gain, base=0, count=LAYERS):
        for step in range(count):
            x = base + step
            even, odd = source_dir[x + 1, 0], source_dir[x + 1, 1]
            c = lambda k, side: coef[x, k, side]
            acc_even = c(0, 0) * source_dir[x + 2, 0] + c(1, 0) * source_dir[x, 0]
            acc_odd = c(0, 1) * source_dir[x + 2, 1] + c(1, 1) * source_dir[x, 1]
            acc_even += c(4, 0) * odd
            acc_odd += c(5, 1) * even
            low = c(5, 0) * odd
            high = c(4, 1) * even
            for s in range(1, THROWS + 1):
                even_ahead, odd_ahead = ahead(even, s), ahead(odd, s)
                even_behind, odd_behind = behind(even, s), behind(odd, s)
                if s == 1:
                    acc_even += c(2, 0) * even_ahead + c(3, 0) * even_behind
                    acc_odd += c(2, 1) * odd_ahead + c(3, 1) * odd_behind
                acc_even += c(5 + s, 0) * odd_ahead
                acc_odd += c(8 + s, 1) * even_behind
                low += c(8 + s, 0) * odd_behind
                high += c(5 + s, 1) * even_ahead
            acc_even += down(low)
            acc_odd += up(high)
            for side, own, acc in ((0, even, acc_even), (1, odd, acc_odd)):
                left = resid[x, side] - (own - acc)
                resid[x, side] = left
                total[x + 1, side] = total[x + 1, side] + own
                target_dir[x + 1, side] = keep * own + gain * left

    def solve(total):
        def pair(i, carry):
            def pick(k, j):
                return jnp.where(
                    i == 0,
                    FACTORS[k][j],
                    jnp.where(i == 1, FACTORS[k + 2][j], FACTORS[k + 4][j]),
                ).astype(jnp.float32)

            sweep(total, dir_a, dir_b, pick(0, 0), pick(0, 1))
            sweep(total, dir_b, dir_a, pick(1, 0), pick(1, 1))
            return carry

        lax.fori_loop(0, SWEEPS // 2, pair, 0)

    solve(field)
    for x in range(LAYERS):
        for side in range(2):
            value = field[x + 1, side] + dir_a[x + 1, side]
            field[x + 1, side] = value
            start = weight[x, side] * (value - data[x, side]) * inverse[x, side]
            resid[x, side] = start
            dir_a[x + 1, side] = start * (1.0 / CENTER)
            adjoint[x + 1, side] = zeros
    for k in range(SWEEPS):
        reach = SWEEPS - k
        count = min(2 * reach + 1, LAYERS)
        base = jnp.clip(here - reach, 0, LAYERS - count)
        pair = (dir_a, dir_b) if k % 2 == 0 else (dir_b, dir_a)
        sweep(adjoint, *pair, *FACTORS[k], base, count)

    def around(ref, extra=None):
        def read(layer):
            pair = [ref[here + layer, 0], ref[here + layer, 1]]
            if extra is not None:
                pair = [pair[k] + extra[here + layer, k] for k in range(2)]
            return pair

        below, mine, above = read(0), read(1), read(2)
        return mine, neighbours(mine[0], mine[1], above, below)

    perm_mine, perm_next = around(perm)
    pres_mine, pres_next = around(field)
    adj_mine, adj_next = around(adjoint, dir_a)
    glogk = []
    for side in range(2):
        total = zeros
        for k in range(12):
            other = perm_next[side][k]
            rate = (
                -(adj_mine[side] - adj_next[side][k])
                * (pres_mine[side] - pres_next[side][k])
                * local[k, side]
                / (perm_mine[side] + other)
            )
            total = total + rate * other
        glogk.append(total)

    def apart(even, odd):
        left = left_half()
        return jnp.where(left, even, swap(odd)), jnp.where(left, swap(even), odd)

    first, second = apart(*pres_mine)
    pressure_ref[0] = first
    pressure_ref[1] = second
    first, second = apart(*glogk)
    first, second = first.astype(jnp.bfloat16), second.astype(jnp.bfloat16)
    for m in range(glogk_ref.shape[0]):
        glogk_ref[m, 0] = first
        glogk_ref[m, 1] = second


def physics(own, other, copies):
    f32 = jnp.float32

    def buffer(*lead):
        return pltpu.VMEM((*lead, ROWS, LANES), f32)

    padded = LAYERS + 2
    return pl.pallas_call(
        physics_kernel,
        in_specs=[VMEM] * 2,
        out_specs=[VMEM, VMEM],
        out_shape=[
            jax.ShapeDtypeStruct((2, ROWS, LANES), f32),
            jax.ShapeDtypeStruct((copies, 2, ROWS, LANES), jnp.bfloat16),
        ],
        scratch_shapes=[
            buffer(padded, 2),
            buffer(LAYERS, 12, 2),
            buffer(LAYERS, 2),
            buffer(12, 2),
            buffer(LAYERS, THROWS, 2),
            buffer(LAYERS, 2),
            buffer(LAYERS, 2),
            buffer(LAYERS, 2),
            buffer(padded, 2),
            buffer(padded, 2),
            buffer(padded, 2),
            buffer(padded, 2),
        ],
        compiler_params=pltpu.CompilerParams(vmem_limit_bytes=12 * 2**20),
        cost_estimate=cost(2**32, 2**24),
        name="physics",
    )(own, other)


def gradient_kernel(glogk_ref, basis_ref, out_ref, rows):
    chains = out_ref.shape[0]
    values = glogk_ref[...].astype(jnp.float32).reshape(chains, ROWS, LANES)
    rows[...] = values
    for row in range(ROWS):
        left = rows[:, row, :].astype(jnp.bfloat16)
        part = jnp.dot(
            left,
            basis_ref[row * LANES : (row + 1) * LANES, :],
            preferred_element_type=jnp.float32,
        )
        total = part if row == 0 else total + part
    out_ref[...] = total.astype(jnp.bfloat16)


def gradient_of(glogk, basis):
    chains = glogk.shape[0] * glogk.shape[1]
    return pl.pallas_call(
        gradient_kernel,
        in_specs=[VMEM, VMEM],
        out_specs=VMEM,
        out_shape=jax.ShapeDtypeStruct((chains, basis.shape[1]), jnp.bfloat16),
        scratch_shapes=[pltpu.VMEM((chains, ROWS, LANES), jnp.float32)],
        compiler_params=pltpu.CompilerParams(vmem_limit_bytes=6 * 2**20),
        cost_estimate=cost(2 * chains * basis.size, 2 * basis.size),
        name="gradient",
    )(glogk, basis)


def copies_kernel(one_ref, two_ref, out_ref):
    total = one_ref[...].astype(jnp.float32) + two_ref[...].astype(jnp.float32)
    total = total.astype(jnp.bfloat16)
    for k in range(out_ref.shape[0]):
        out_ref[k] = total


def copies_of(one, two, count):
    return pl.pallas_call(
        copies_kernel,
        in_specs=[VMEM, VMEM],
        out_specs=VMEM,
        out_shape=jax.ShapeDtypeStruct((count, *one.shape), jnp.bfloat16),
        cost_estimate=cost(2**16, 2**19),
        compiler_params=pltpu.CompilerParams(vmem_limit_bytes=4 * 2**20),
        name="copies",
    )(one, two)


def exchange(value, mask, size):
    return lax.ppermute(value, AXES, [(i, i ^ mask) for i in range(size)])


def body(
    theta,
    basis,
    mean_logk,
    face_mult,
    storage,
    sources,
    obs_data,
    obs_weight,
    fault_pairs,
    fault_mult,
    noise,
):
    modes_n, cells_n = lax.axis_size("modes"), lax.axis_size("cells")
    size = cells_n * modes_n

    partial_field = field_of(theta.T, basis).reshape(modes_n, 2, ROWS, LANES)
    parts = lax.all_to_all(partial_field, "modes", 0, 0)
    pieces = combine(
        parts,
        mean_logk.reshape(ROWS, LANES),
        face_mult,
        storage.reshape(ROWS, LANES),
        sources.reshape(ROWS, LANES),
        obs_data.reshape(ROWS, LANES),
        obs_weight.reshape(ROWS, LANES),
        fault_pairs.T,
        fault_mult.reshape(1, SLOT_ROWS * LANES),
    )
    groups = [
        [(r + turn(m)) % cells_n * modes_n + m for r in range(cells_n)] for m in range(modes_n)
    ]
    pieces = lax.all_to_all(pieces, AXES, 0, 0, axis_index_groups=groups)
    others = exchange(pieces, 1, size)
    pressure, glogk = physics(pieces, others, modes_n)
    glogk = lax.all_to_all(glogk, "modes", 0, 0)
    grad_rows = gradient_of(glogk, basis)
    half = cells_n // 2
    grad_rows = copies_of(grad_rows, exchange(grad_rows, half * modes_n, size), half)
    groups = [
        [(side + (r + turn(m)) % half) * modes_n + m for r in range(half)]
        for m in range(modes_n)
        for side in (0, half)
    ]
    grad_rows = lax.all_to_all(grad_rows, AXES, 0, 0, axis_index_groups=groups)
    grad = jnp.sum(grad_rows.astype(jnp.float32), 0).T
    theta_next = theta - STEP_SIZE * (grad + theta) + math.sqrt(2.0 * STEP_SIZE) * noise
    return (theta_next, grad, pressure.reshape(2, NY * NZ))


def solution(mesh):
    return jax.shard_map(
        body,
        mesh=mesh,
        in_specs=(
            P("modes", None),
            P("cells", "modes"),
            P("cells"),
            P(None, "cells"),
            P("cells"),
            P("cells"),
            P("cells"),
            P("cells"),
            P("cells", None),
            P("cells"),
            P("modes", None),
        ),
        out_specs=(P("modes", None), P("modes", None), P("modes", "cells")),
        check_vma=False,
    )
```

```python
import math

import jax
import jax.numpy as jnp
from jax import lax
from jax.experimental import pallas as pl
from jax.experimental.pallas import tpu as pltpu
from jax.sharding import PartitionSpec as P

NY = 32
NZ = 64
SWEEPS = 6
LAYERS = 16
LANES = 128
ROWS = NY * NZ // LANES
SLOT_ROWS = 2
PIECE = 48
THROWS = 3

LOW_EIG = 0.1
HIGH_EIG = 1.9
STEP_SIZE = 0.01
AXES = ("cells", "modes")
VMEM = pl.BlockSpec(memory_space=pltpu.VMEM)


def place():
    return lax.axis_index("cells"), lax.axis_index("modes") & 1


def turn(mode):
    return mode


def cost(flops, bytes_accessed):
    return pl.CostEstimate(flops=flops, bytes_accessed=bytes_accessed, transcendentals=0)


def chebyshev():
    center = 0.5 * (HIGH_EIG + LOW_EIG)
    half = 0.5 * (HIGH_EIG - LOW_EIG)
    sigma = center / half
    rho = 1.0 / sigma
    factors = []
    for _ in range(SWEEPS):
        rho_next = 1.0 / (2.0 * sigma - rho)
        factors.append((rho_next * rho, 2.0 * rho_next / half))
        rho = rho_next
    return center, factors


CENTER, FACTORS = chebyshev()


def field_kernel(theta_hbm, basis_hbm, out_ref, theta, basis, sems):
    steps = sems.shape[0] - 1
    count = basis.shape[0] // steps
    copies = [pltpu.make_async_copy(theta_hbm, theta, sems.at[steps])]
    for step in range(steps):
        rows = pl.ds(step * count, count)
        copies.append(pltpu.make_async_copy(basis_hbm.at[rows], basis.at[rows], sems.at[step]))
    for copy in copies:
        copy.start()
    copies[0].wait()
    theta_b = theta[...].astype(jnp.bfloat16)
    for step in range(steps):
        copies[step + 1].wait()
        part = lax.dot_general(
            theta_b,
            basis[step * count : (step + 1) * count, :],
            (((1,), (1,)), ((), ())),
            preferred_element_type=jnp.float32,
        )
        for row in range(count // LANES):
            out_ref[:, step * (count // LANES) + row, :] = part[:, row * LANES : (row + 1) * LANES]


def field_of(theta, basis):
    chains, modes = theta.shape
    steps = 2
    return pl.pallas_call(
        field_kernel,
        in_specs=[pl.BlockSpec(memory_space=pltpu.HBM)] * 2,
        out_specs=VMEM,
        out_shape=jax.ShapeDtypeStruct((chains, ROWS, LANES), jnp.float32),
        scratch_shapes=[
            pltpu.VMEM(theta.shape, theta.dtype),
            pltpu.VMEM(basis.shape, basis.dtype),
            pltpu.SemaphoreType.DMA((steps + 1,)),
        ],
        cost_estimate=cost(2 * chains * modes * ROWS * LANES, 2 * modes * ROWS * LANES),
        compiler_params=pltpu.CompilerParams(vmem_limit_bytes=8 * 2**20),
        name="field",
    )(
        pltpu.with_memory_space_constraint(theta, pltpu.HBM),
        pltpu.with_memory_space_constraint(basis, pltpu.HBM),
    )


def left_half():
    return lax.broadcasted_iota(jnp.int32, (ROWS, LANES), 1) < NZ


def swap(a):
    return pltpu.roll(a, NZ, 1)


def span(low, high):
    return low, (high - low) / 65535.0


MULT_SPAN, STORE_SPAN, WELL_SPAN, UNIT_SPAN = (
    span(0.3, 3.0),
    span(0.05, 0.5),
    span(-6.0, 6.0),
    span(0.1, 1.0),
)


def code16(a, within):
    low, step = within
    return ((a - low) * (1.0 / step) + 0.5).astype(jnp.int32) - 32768


def value16(code, within):
    low, step = within
    return (code + 32768).astype(jnp.float32) * step + low


def pack(high, low):
    return (high << 16) | (low & 0xFFFF)


def high16(word):
    return word >> 16


def low16(word):
    return (word << 16) >> 16


def combine_kernel(
    parts_ref,
    mean_ref,
    face_ref,
    storage_ref,
    sources_ref,
    data_ref,
    weight_ref,
    pairs_ref,
    fault_ref,
    out_ref,
):
    total = jnp.sum(parts_ref[...], axis=0)
    mean = mean_ref[...]
    first, second = total[0] + mean, total[1] + mean
    left = left_half()
    even = jnp.where(left, first, swap(second))
    odd = jnp.where(left, swap(first), second)
    top = jnp.max(jnp.maximum(jnp.abs(even), jnp.abs(odd)), axis=(0, 1), keepdims=True)
    bound = (top * 256.0).astype(jnp.int32) + 1
    factor = (32767.0 * 256.0) / bound.astype(jnp.float32)

    def scaled(a):
        return jnp.floor(a * factor + 0.5).astype(jnp.int32)

    def rows_of(a):
        return jnp.concatenate(
            [a[:, row * LANES : (row + 1) * LANES] for row in range(a.shape[1] // LANES)], 0
        )

    face = face_ref[...]
    mult = [code16(rows_of(face[k : k + 1]), MULT_SPAN) for k in range(3)]
    store = code16(storage_ref[...], STORE_SPAN)
    source = code16(sources_ref[...], WELL_SPAN)
    data = code16(data_ref[...], WELL_SPAN)
    weight = code16(weight_ref[...], UNIT_SPAN)
    near, far = rows_of(pairs_ref[0:1]), rows_of(pairs_ref[1:2])
    code = near * 4 + jnp.where(near == far, 0, far - near - NZ)
    fault = (rows_of(fault_ref[...]) * 65535.0 + 0.5).astype(jnp.int32) - 32768
    bounds = jnp.broadcast_to(bound, (2, LANES))
    zeros = jnp.zeros((2, LANES), jnp.int32)
    forms = (
        [
            pack(mult[0], mult[1]),
            pack(mult[2][0:8], mult[2][8:16]),
            pack(store[0:4], store[4:8]),
            zeros,
            bounds,
        ],
        [
            pack(source, data),
            pack(weight[0:8], weight[8:16]),
            pack(store[8:12], store[12:16]),
            pack(code, fault),
            bounds,
        ],
    )
    forms = [jnp.concatenate(form, 0) for form in forms]
    fixed = jnp.where(place()[1] == 0, forms[0], forms[1])
    field = pack(scaled(even), scaled(odd))
    for k in range(out_ref.shape[0]):
        out_ref[k, 0:ROWS] = field
        out_ref[k, ROWS:PIECE] = fixed


def combine(parts, *fixed):
    return pl.pallas_call(
        combine_kernel,
        in_specs=[VMEM] * (1 + len(fixed)),
        out_specs=VMEM,
        out_shape=jax.ShapeDtypeStruct((LAYERS, PIECE, LANES), jnp.int32),
        cost_estimate=cost(2**17, 2**20),
        compiler_params=pltpu.CompilerParams(vmem_limit_bytes=4 * 2**20),
        name="combine",
    )(parts, *fixed)


def harmonic(left, right):
    return 2.0 * left * right / (left + right)


def ahead(a, s):
    return pltpu.roll(a, LANES - s, 1)


def behind(a, s):
    return pltpu.roll(a, s, 1)


def up(a):
    return pltpu.roll(a, ROWS - 1, 0)


def down(a):
    return pltpu.roll(a, 1, 0)


def spread(a):
    left, other = left_half(), swap(a)
    return jnp.where(left, a, other), jnp.where(left, other, a)


def neighbours(even, odd, above, below):
    to_even = [above[0], below[0], ahead(even, 1), behind(even, 1), odd, down(odd)]
    to_odd = [above[1], below[1], ahead(odd, 1), behind(odd, 1), up(even), even]
    for s in range(1, THROWS + 1):
        to_even.append(ahead(odd, s))
        to_odd.append(up(ahead(even, s)))
    for s in range(1, THROWS + 1):
        to_even.append(down(behind(odd, s)))
        to_odd.append(behind(even, s))
    return to_even, to_odd


def physics_kernel(
    own_ref,
    other_ref,
    pressure_ref,
    glogk_ref,
    perm,
    coef,
    inverse,
    local,
    fault,
    weight,
    data,
    resid,
    field,
    adjoint,
    dir_a,
    dir_b,
):
    here, core = place()
    mode = lax.axis_index("modes")
    own_turn, other_turn = turn(mode), turn(mode ^ 1)

    def own_at(x):
        return (x - own_turn) & (LAYERS - 1)

    def other_at(x):
        return (x - other_turn) & (LAYERS - 1)

    zeros = jnp.zeros((ROWS, LANES), jnp.float32)
    for pad in (0, LAYERS + 1):
        for k in range(2):
            perm[pad, k] = zeros + 1.0
            field[pad, k] = zeros
            adjoint[pad, k] = zeros
            dir_a[pad, k] = zeros
            dir_b[pad, k] = zeros
    for x in range(LAYERS):
        word = own_ref[own_at(x), 0:ROWS]
        factor = own_ref[own_at(x), PIECE - 1 : PIECE].astype(jnp.float32) * (1.0 / (32767.0 * 256.0))
        perm[x + 1, 0] = jnp.exp(high16(word).astype(jnp.float32) * factor)
        perm[x + 1, 1] = jnp.exp(low16(word).astype(jnp.float32) * factor)

    lane = lax.broadcasted_iota(jnp.int32, (ROWS, LANES), 1)
    row = lax.broadcasted_iota(jnp.int32, (ROWS, LANES), 0)
    z_inside = (lane & (NZ - 1)) < NZ - 1
    y_inside = row < ROWS - 1
    keys = lax.broadcasted_iota(jnp.int32, (THROWS * ROWS, SLOT_ROWS * LANES), 0)
    lanes_of = lax.broadcasted_iota(jnp.int32, (LANES, SLOT_ROWS * LANES), 0)

    def join(x):
        own = own_ref[own_at(x), PIECE - 4 : PIECE - 2]
        other = other_ref[other_at(x), PIECE - 4 : PIECE - 2]
        slots = jnp.where(core == 0, other, own)
        slots = jnp.concatenate([slots[h : h + 1] for h in range(SLOT_ROWS)], 1)
        code, amount = high16(slots), low16(slots) + 32768
        throw, cell = code & 3, code >> 2
        key = jnp.where(throw > 0, (throw - 1) * ROWS + (cell >> 7), -1)
        hit = keys == key
        parts = [
            jnp.where(hit, part.astype(jnp.float32), 0.0) for part in (amount >> 8, amount & 255)
        ]
        rows_hot = jnp.concatenate(parts, 0).astype(jnp.bfloat16)
        lanes_hot = jnp.where(lanes_of == (cell & (LANES - 1)), 1.0, 0.0).astype(jnp.bfloat16)
        sums = lax.dot_general(
            rows_hot, lanes_hot, (((1,), (1,)), ((), ())), preferred_element_type=jnp.float32
        )
        count = THROWS * ROWS
        total = (sums[:count] * 256.0 + sums[count:]) * (1.0 / 65535.0)
        for s in range(THROWS):
            even, odd = spread(total[s * ROWS : (s + 1) * ROWS])
            fault[x, s, 0] = even
            fault[x, s, 1] = odd

    for x in range(LAYERS):
        join(x)

    def prepare(x, carry):
        own, other = own_ref[own_at(x), ROWS:PIECE], other_ref[other_at(x), ROWS:PIECE]
        first = jnp.where(core == 0, own, other)
        second = jnp.where(core == 0, other, own)
        mult_x = spread(value16(high16(first[0:16]), MULT_SPAN))
        mult_y = spread(value16(low16(first[0:16]), MULT_SPAN))
        halves = (high16(first[16:24]), low16(first[16:24]))
        mult_z = spread(value16(jnp.concatenate(halves, 0), MULT_SPAN))
        store = [op(w[24:28]) for w in (first, second) for op in (high16, low16)]
        storage = spread(value16(jnp.concatenate(store, 0), STORE_SPAN))
        source = spread(value16(high16(second[0:16]), WELL_SPAN))
        obs_data = spread(value16(low16(second[0:16]), WELL_SPAN))
        halves = (high16(second[16:24]), low16(second[16:24]))
        obs_weight = spread(value16(jnp.concatenate(halves, 0), UNIT_SPAN))
        even, odd = perm[x + 1, 0], perm[x + 1, 1]
        inside = jnp.where(x < LAYERS - 1, 1.0, 0.0)
        xp_even = harmonic(even, perm[x + 2, 0]) * mult_x[0] * inside
        xp_odd = harmonic(odd, perm[x + 2, 1]) * mult_x[1] * inside
        xm_even, xm_odd = carry
        zp_even = jnp.where(z_inside, harmonic(even, ahead(even, 1)) * mult_z[0], 0.0)
        zp_odd = jnp.where(z_inside, harmonic(odd, ahead(odd, 1)) * mult_z[1], 0.0)
        y_even = harmonic(even, odd) * mult_y[0]
        y_odd = jnp.where(y_inside, harmonic(odd, up(even)) * mult_y[1], 0.0)
        to_even = [xp_even, xm_even, zp_even, behind(zp_even, 1), y_even, down(y_odd)]
        to_odd = [xp_odd, xm_odd, zp_odd, behind(zp_odd, 1), y_odd, y_even]
        back_even, back_odd = [], []
        for s in range(1, THROWS + 1):
            fault_even = harmonic(even, ahead(odd, s)) * fault[x, s - 1, 0]
            fault_odd = harmonic(odd, up(ahead(even, s))) * fault[x, s - 1, 1]
            to_even.append(fault_even)
            to_odd.append(fault_odd)
            back_even.append(down(behind(fault_odd, s)))
            back_odd.append(behind(fault_even, s))
        to_even += back_even
        to_odd += back_odd

        @pl.when(x == here)
        def _():
            for k in range(12):
                local[k, 0] = to_even[k]
                local[k, 1] = to_odd[k]

        for side, trans in ((0, to_even), (1, to_odd)):
            diag = storage[side]
            for t in trans:
                diag = diag + t
            inv = 1.0 / diag
            inverse[x, side] = inv
            for k in range(12):
                value = trans[k] * inv
                if side == 0 and k in (5, 9, 10, 11):
                    value = up(value)
                if side == 1 and k in (4, 6, 7, 8):
                    value = down(value)
                coef[x, k, side] = value
            weight[x, side] = obs_weight[side]
            data[x, side] = obs_data[side]
            start = source[side] * inv
            resid[x, side] = start
            dir_a[x + 1, side] = start * (1.0 / CENTER)
            field[x + 1, side] = zeros
        return xp_even, xp_odd

    lax.fori_loop(0, LAYERS, prepare, (zeros, zeros), unroll=4)

    def sweep(total, source_dir, target_dir, keep, gain, base=0, count=LAYERS):
        for step in range(count):
            x = base + step
            even, odd = source_dir[x + 1, 0], source_dir[x + 1, 1]
            c = lambda k, side: coef[x, k, side]
            acc_even = c(0, 0) * source_dir[x + 2, 0] + c(1, 0) * source_dir[x, 0]
            acc_odd = c(0, 1) * source_dir[x + 2, 1] + c(1, 1) * source_dir[x, 1]
            acc_even += c(4, 0) * odd
            acc_odd += c(5, 1) * even
            low = c(5, 0) * odd
            high = c(4, 1) * even
            for s in range(1, THROWS + 1):
                even_ahead, odd_ahead = ahead(even, s), ahead(odd, s)
                even_behind, odd_behind = behind(even, s), behind(odd, s)
                if s == 1:
                    acc_even += c(2, 0) * even_ahead + c(3, 0) * even_behind
                    acc_odd += c(2, 1) * odd_ahead + c(3, 1) * odd_behind
                acc_even += c(5 + s, 0) * odd_ahead
                acc_odd += c(8 + s, 1) * even_behind
                low += c(8 + s, 0) * odd_behind
                high += c(5 + s, 1) * even_ahead
            acc_even += down(low)
            acc_odd += up(high)
            for side, own, acc in ((0, even, acc_even), (1, odd, acc_odd)):
                left = resid[x, side] - (own - acc)
                resid[x, side] = left
                total[x + 1, side] = total[x + 1, side] + own
                target_dir[x + 1, side] = keep * own + gain * left

    def solve(total):
        def pair(i, carry):
            def pick(k, j):
                return jnp.where(
                    i == 0,
                    FACTORS[k][j],
                    jnp.where(i == 1, FACTORS[k + 2][j], FACTORS[k + 4][j]),
                ).astype(jnp.float32)

            sweep(total, dir_a, dir_b, pick(0, 0), pick(0, 1))
            sweep(total, dir_b, dir_a, pick(1, 0), pick(1, 1))
            return carry

        lax.fori_loop(0, SWEEPS // 2, pair, 0)

    solve(field)
    for x in range(LAYERS):
        for side in range(2):
            value = field[x + 1, side] + dir_a[x + 1, side]
            field[x + 1, side] = value
            start = weight[x, side] * (value - data[x, side]) * inverse[x, side]
            resid[x, side] = start
            dir_a[x + 1, side] = start * (1.0 / CENTER)
            adjoint[x + 1, side] = zeros
    for k in range(SWEEPS):
        reach = SWEEPS - k
        count = min(2 * reach + 1, LAYERS)
        base = jnp.clip(here - reach, 0, LAYERS - count)
        pair = (dir_a, dir_b) if k % 2 == 0 else (dir_b, dir_a)
        sweep(adjoint, *pair, *FACTORS[k], base, count)

    def around(ref, extra=None):
        def read(layer):
            pair = [ref[here + layer, 0], ref[here + layer, 1]]
            if extra is not None:
                pair = [pair[k] + extra[here + layer, k] for k in range(2)]
            return pair

        below, mine, above = read(0), read(1), read(2)
        return mine, neighbours(mine[0], mine[1], above, below)

    perm_mine, perm_next = around(perm)
    pres_mine, pres_next = around(field)
    adj_mine, adj_next = around(adjoint, dir_a)
    glogk = []
    for side in range(2):
        total = zeros
        for k in range(12):
            other = perm_next[side][k]
            rate = (
                -(adj_mine[side] - adj_next[side][k])
                * (pres_mine[side] - pres_next[side][k])
                * local[k, side]
                / (perm_mine[side] + other)
            )
            total = total + rate * other
        glogk.append(total)

    def apart(even, odd):
        left = left_half()
        return jnp.where(left, even, swap(odd)), jnp.where(left, swap(even), odd)

    first, second = apart(*pres_mine)
    pressure_ref[0] = first
    pressure_ref[1] = second
    first, second = apart(*glogk)
    first, second = first.astype(jnp.bfloat16), second.astype(jnp.bfloat16)
    for m in range(glogk_ref.shape[0]):
        glogk_ref[m, 0] = first
        glogk_ref[m, 1] = second


def physics(own, other, copies):
    f32 = jnp.float32

    def buffer(*lead):
        return pltpu.VMEM((*lead, ROWS, LANES), f32)

    padded = LAYERS + 2
    return pl.pallas_call(
        physics_kernel,
        in_specs=[VMEM] * 2,
        out_specs=[VMEM, VMEM],
        out_shape=[
            jax.ShapeDtypeStruct((2, ROWS, LANES), f32),
            jax.ShapeDtypeStruct((copies, 2, ROWS, LANES), jnp.bfloat16),
        ],
        scratch_shapes=[
            buffer(padded, 2),
            buffer(LAYERS, 12, 2),
            buffer(LAYERS, 2),
            buffer(12, 2),
            buffer(LAYERS, THROWS, 2),
            buffer(LAYERS, 2),
            buffer(LAYERS, 2),
            buffer(LAYERS, 2),
            buffer(padded, 2),
            buffer(padded, 2),
            buffer(padded, 2),
            buffer(padded, 2),
        ],
        compiler_params=pltpu.CompilerParams(vmem_limit_bytes=12 * 2**20),
        cost_estimate=cost(2**32, 2**24),
        name="physics",
    )(own, other)


def gradient_kernel(glogk_ref, basis_ref, out_ref, rows):
    chains = out_ref.shape[0]
    values = glogk_ref[...].astype(jnp.float32).reshape(chains, ROWS, LANES)
    rows[...] = values
    for row in range(ROWS):
        left = rows[:, row, :].astype(jnp.bfloat16)
        part = jnp.dot(
            left,
            basis_ref[row * LANES : (row + 1) * LANES, :],
            preferred_element_type=jnp.float32,
        )
        total = part if row == 0 else total + part
    out_ref[...] = total.astype(jnp.bfloat16)


def gradient_of(glogk, basis):
    chains = glogk.shape[0] * glogk.shape[1]
    return pl.pallas_call(
        gradient_kernel,
        in_specs=[VMEM, VMEM],
        out_specs=VMEM,
        out_shape=jax.ShapeDtypeStruct((chains, basis.shape[1]), jnp.bfloat16),
        scratch_shapes=[pltpu.VMEM((chains, ROWS, LANES), jnp.float32)],
        compiler_params=pltpu.CompilerParams(vmem_limit_bytes=6 * 2**20),
        cost_estimate=cost(2 * chains * basis.size, 2 * basis.size),
        name="gradient",
    )(glogk, basis)


def copies_kernel(one_ref, two_ref, out_ref):
    total = one_ref[...].astype(jnp.float32) + two_ref[...].astype(jnp.float32)
    total = total.astype(jnp.bfloat16)
    for k in range(out_ref.shape[0]):
        out_ref[k] = total


def copies_of(one, two, count):
    return pl.pallas_call(
        copies_kernel,
        in_specs=[VMEM, VMEM],
        out_specs=VMEM,
        out_shape=jax.ShapeDtypeStruct((count, *one.shape), jnp.bfloat16),
        cost_estimate=cost(2**16, 2**19),
        compiler_params=pltpu.CompilerParams(vmem_limit_bytes=4 * 2**20),
        name="copies",
    )(one, two)


def exchange(value, mask, size):
    return lax.ppermute(value, AXES, [(i, i ^ mask) for i in range(size)])


def body(
    theta,
    basis,
    mean_logk,
    face_mult,
    storage,
    sources,
    obs_data,
    obs_weight,
    fault_pairs,
    fault_mult,
    noise,
):
    modes_n, cells_n = lax.axis_size("modes"), lax.axis_size("cells")
    size = cells_n * modes_n

    partial_field = field_of(theta.T, basis).reshape(modes_n, 2, ROWS, LANES)
    parts = lax.all_to_all(partial_field, "modes", 0, 0)
    pieces = combine(
        parts,
        mean_logk.reshape(ROWS, LANES),
        face_mult,
        storage.reshape(ROWS, LANES),
        sources.reshape(ROWS, LANES),
        obs_data.reshape(ROWS, LANES),
        obs_weight.reshape(ROWS, LANES),
        fault_pairs.T,
        fault_mult.reshape(1, SLOT_ROWS * LANES),
    )
    groups = [
        [(r + turn(m)) % cells_n * modes_n + m for r in range(cells_n)] for m in range(modes_n)
    ]
    pieces = lax.all_to_all(pieces, AXES, 0, 0, axis_index_groups=groups)
    others = exchange(pieces, 1, size)
    pressure, glogk = physics(pieces, others, modes_n)
    glogk = lax.all_to_all(glogk, "modes", 0, 0)
    grad_rows = gradient_of(glogk, basis)
    half = cells_n // 2
    grad_rows = copies_of(grad_rows, exchange(grad_rows, half * modes_n, size), half)
    groups = [
        [(side + (r + turn(m)) % half) * modes_n + m for r in range(half)]
        for m in range(modes_n)
        for side in (0, half)
    ]
    grad_rows = lax.all_to_all(grad_rows, AXES, 0, 0, axis_index_groups=groups)
    grad = jnp.sum(grad_rows.astype(jnp.float32), 0).T
    theta_next = theta - STEP_SIZE * (grad + theta) + math.sqrt(2.0 * STEP_SIZE) * noise
    return (theta_next, grad, pressure.reshape(2, NY * NZ))


def solution(mesh):
    return jax.shard_map(
        body,
        mesh=mesh,
        in_specs=(
            P("modes", None),
            P("cells", "modes"),
            P("cells"),
            P(None, "cells"),
            P("cells"),
            P("cells"),
            P("cells"),
            P("cells"),
            P("cells", None),
            P("cells"),
            P("modes", None),
        ),
        out_specs=(P("modes", None), P("modes", None), P("modes", "cells")),
        check_vma=False,
    )
```
